32 devices in a mesh: vert: 8 (over z, x), tm: 4 (over y, core).
Axes of the slice: x: 2, y: 2, z: 4, core: 2. Of those that a mesh axis runs over, the one named last changes fastest.
Arguments:
- source: bfloat16 [10240, 512], P('vert', 'tm'), may hold values from -6 to 6
- band_taps: bfloat16 [2, 2, 65], replicated, may hold values from -0.75 to 0.75
- smooth_taps: bfloat16 [2, 65], replicated, may hold values from 0.0009 to 0.031
- parcel_ids: int32 [3, 10240], P(None, 'vert'), may hold values from 0 to 999, as said below
Outputs:
- envelope_coupling: float32 [4, 2, 1504, 1504], P('tm', None, 'vert')
The draws below stay inside these ranges and needn't reach their ends.
Inputs may be any that keep to these rules, and one draw needn't show every extreme that they name: `parcel_ids`: row r = 0, 1, 2 gives each vertex's parcel in the atlas of 100, 400 or 1000 parcels (values below that count); every parcel of each atlas has at least one vertex.
All inputs are finite; a program needn't handle non-finite values.
Results may differ from the reference program's by a relative error of at most 0.0053.
Values may be sent and summed in bfloat16 or wider, within the bound.
No kernel may reach another device: no remote copies, remote signals or barrier semaphores. Data moves between devices by JAX's collectives and lax.ppermute only.
A program may use at most 64 MiB of HBM per device.

```python
import jax
import jax.numpy as jnp
from jax import lax

P1 = 100
P2 = 400
P3 = 1000
BANDS = 2
TAPS = 65
HALF = 32
LAG = 64
LAG_STEP = 1
NLAG = 129
VERT_DEV = 1280
T_DEV = 128
VERTICES = 10240
TIMES = 512
PAR = 1504
N_VERT = 8
N_TM = 4


def draw_parcel_ids(key, part):
    levels = []
    for level, limit in enumerate((P1, P2, P3)):
        branch = jax.random.fold_in(key, 11 + level)
        first_key, second_key, third_key = jax.random.split(branch, 3)
        order = jax.random.permutation(first_key, VERTICES).astype(jnp.int32)
        left = jax.random.randint(second_key, (VERTICES,), 0, limit)
        right = jax.random.randint(third_key, (VERTICES,), 0, limit)
        levels.append(jnp.where(order < limit, order, jnp.minimum(left, right)))
    return jnp.stack(levels).astype(jnp.int32)


def draw_smooth_taps(key, part):
    branch = jax.random.fold_in(key, 29)
    phase_key, second_key, rough_key, floor_key = jax.random.split(branch, 4)
    phases = jax.random.randint(phase_key, (BANDS, 1), 0, 4).astype(jnp.int32)
    seconds = jax.random.randint(second_key, (BANDS, 1), 0, 8).astype(jnp.int32)
    position = jnp.arange(TAPS, dtype=jnp.int32)[None, :]
    comb = ((position + phases) % 4 == 0).astype(jnp.float32)
    sparse = ((position + seconds) % 8 == 0).astype(jnp.float32)
    pattern = jnp.maximum(comb, 0.6 * sparse)
    rough = jax.random.uniform(rough_key, (BANDS, TAPS), jnp.float32)
    floor_draw = jax.random.uniform(floor_key, (BANDS, TAPS), jnp.float32)
    peak = 0.6 + 0.4 * rough
    floor_level = 0.001 + 0.002 * floor_draw
    values = floor_level + 0.027 * pattern * peak
    return values.astype(jnp.float32).astype(jnp.bfloat16)


def shard_levels(stream_key, shape, shards, low, high):
    loudness, own = 1.0, jax.random.fold_in(stream_key, 6)
    for dim, shards_of in shards:
        heights = jnp.exp(jax.random.uniform(jax.random.fold_in(own, dim), (shards_of,), jnp.float32, low / len(shards), high / len(shards)))
        loudness = loudness * jnp.repeat(heights, shape[dim] // shards_of).reshape([-1 if axis == dim else 1 for axis in range(len(shape))])
    return loudness


def bell_draw(stream_key, extent, scale, most, pieces=(), kind=jnp.bfloat16):
    values = scale * jax.random.normal(stream_key, extent, jnp.float32)
    if pieces:
        values = values * shard_levels(stream_key, extent, pieces, -0.22, 0.18)
    return jnp.clip(values, -most, most).astype(kind)


def setup_inputs(seed: int = 0) -> dict:
    arg_keys = jax.random.split(jax.random.key(seed), 5)
    source = bell_draw(arg_keys[0], (VERTICES, TIMES), 1.0, 6.0, ((0, 8), (1, 4)))
    band_taps = bell_draw(arg_keys[1], (2, BANDS, TAPS), TAPS ** -0.5, 0.75)
    smooth_taps = draw_smooth_taps(jax.random.fold_in(arg_keys[4], 71), 0)
    parcel_ids = draw_parcel_ids(jax.random.fold_in(arg_keys[4], 71), 0)
    return dict(source=source, band_taps=band_taps, smooth_taps=smooth_taps, parcel_ids=parcel_ids)


EPSILON = 1e-05

def resolution_of(parcel):
    first = (parcel >= P1).astype(jnp.int32)
    second = (parcel >= P1 + P2).astype(jnp.int32)
    third = (parcel >= P1 + P2 + P3).astype(jnp.int32)
    return first + second + third

def envelopes_of(padded_tile, band_taps, smooth_taps):
    kernels = band_taps.astype(jnp.float32).reshape(2 * BANDS, 1, TAPS)
    wave = lax.conv_general_dilated(padded_tile.astype(jnp.float32)[:, None, :], kernels, (1,), 'VALID', dimension_numbers=('NCH', 'OIH', 'NCH'), precision=lax.Precision.HIGHEST)
    wave = wave.reshape(padded_tile.shape[0], 2, BANDS, TIMES + 2 * HALF)
    power = (wave[:, 0] * wave[:, 0] + wave[:, 1] * wave[:, 1]).astype(jnp.bfloat16)
    smooth = lax.conv_general_dilated(power.astype(jnp.float32), smooth_taps.astype(jnp.float32)[:, None, :], (1,), 'VALID', dimension_numbers=('NCH', 'OIH', 'NCH'), feature_group_count=BANDS, precision=lax.Precision.HIGHEST)
    return smooth.astype(jnp.bfloat16)

def reference(source, band_taps, smooth_taps, parcel_ids):
    padded = jnp.pad(source, ((0, 0), (2 * HALF, 2 * HALF)))
    offsets = jnp.array([0, P1, P1 + P2], dtype=jnp.int32)
    global_ids = (parcel_ids + offsets[:, None]).astype(jnp.int32)
    tiles = padded.reshape(N_VERT, VERT_DEV, TIMES + 4 * HALF)
    id_tiles = global_ids.reshape(3, N_VERT, VERT_DEV).transpose(1, 0, 2)

    def add_tile(sums, pair):
        tile, tile_ids = pair
        envelope = envelopes_of(tile, band_taps, smooth_taps).astype(jnp.float32).reshape(VERT_DEV, BANDS * TIMES)
        for level in range(3):
            sums = sums + jax.ops.segment_sum(envelope, tile_ids[level], num_segments=PAR)
        return (sums, None)
    sums = lax.scan(add_tile, jnp.zeros((PAR, BANDS * TIMES), jnp.float32), (tiles, id_tiles))[0]
    parcel_env = sums.reshape(PAR, BANDS, TIMES)
    extended = jnp.pad(parcel_env, ((0, 0), (0, 0), (LAG, LAG)))
    level_rows = resolution_of(jnp.arange(PAR, dtype=jnp.int32))
    same = ((level_rows[:, None] == level_rows[None, :]) & (level_rows[:, None] < 3)).astype(jnp.float32)

    def one_window(window):
        start = (window * T_DEV).astype(jnp.int32)
        part = lax.dynamic_slice_in_dim(extended, start, T_DEV + 2 * LAG, 2).astype(jnp.float32)
        level_mean = lax.optimization_barrier(jnp.mean(part[:, :, LAG:LAG + T_DEV], axis=2, keepdims=True))
        rounded = lax.optimization_barrier((part - level_mean).astype(jnp.bfloat16))
        centered = rounded.astype(jnp.float32)
        middle = centered[:, :, LAG:LAG + T_DEV]
        spread = lax.rsqrt(lax.optimization_barrier(jnp.mean(middle * middle, axis=2)) + EPSILON).T

        def add_lag(total, lag_idx):
            shifted = lax.dynamic_slice_in_dim(centered, (lag_idx * LAG_STEP).astype(jnp.int32), T_DEV, 2)
            inner = jnp.einsum('ibt,jbt->bij', middle, shifted, precision=lax.Precision.HIGHEST) / T_DEV
            corr = inner * spread[:, :, None] * spread[:, None, :]
            return (total + corr * corr, None)
        energy = lax.scan(add_lag, jnp.zeros((BANDS, PAR, PAR), jnp.float32), jnp.arange(NLAG, dtype=jnp.int32))[0]
        return energy / NLAG * same[None]
    return lax.map(one_window, jnp.arange(N_TM, dtype=jnp.int32))
```

```python
from functools import partial
import math

import numpy as np

import jax
import jax.numpy as jnp
from jax import lax
from jax.experimental import pallas as pl
from jax.experimental.pallas import tpu as pltpu
from jax.sharding import PartitionSpec as P

P1 = 100
P2 = 400
P3 = 1000
BANDS = 2
TAPS = 65
HALF = 32
LAG = 64
LAG_STEP = 1
NLAG = 129


EPSILON = 1e-05


def extended_2(cells, sides, width):
    for axis, dim in sides:
        count = lax.axis_size(axis)
        ends = count - 1
        head = lax.slice_in_dim(cells, 0, width, axis=dim)
        tail = lax.slice_in_dim(cells, cells.shape[dim] - width, cells.shape[dim], axis=dim)
        cells = jnp.concatenate(
            [
                lax.ppermute(tail, axis, [(i, (i + 1) % count) for i in range(ends)]),
                cells,
                lax.ppermute(head, axis, [((i + 1) % count, i) for i in range(ends)]),
            ],
            axis=dim,
        )
    return cells


def toeplitz_band(taps, n_out, n_in):
    period = jnp.concatenate([taps, jnp.zeros((n_in + 1 - taps.shape[0],), taps.dtype)])
    return jnp.tile(period, n_out)[: n_out * n_in].reshape(n_out, n_in)


def resolution_of(parcel):
    first = (parcel >= P1).astype(jnp.int32)
    second = (parcel >= P1 + P2).astype(jnp.int32)
    third = (parcel >= P1 + P2 + P3).astype(jnp.int32)
    return first + second + third


def centered_rows(extended, length):
    level_mean = jnp.mean(extended[:, :, LAG : LAG + length], axis=2, keepdims=True)
    centered = (extended - level_mean).astype(jnp.bfloat16)
    middle = centered[:, :, LAG : LAG + length]
    middle_wide = middle.astype(jnp.float32)
    spread = lax.rsqrt(jnp.mean(middle_wide * middle_wide, axis=2) + EPSILON)
    return (centered, middle, spread)


GROUP = (P1 + P2 + 127) // 128 * 128
TILE = 256
PERIOD = 127
HIGH = lax.Precision.HIGHEST
BF16 = jnp.bfloat16
F32 = jnp.float32


def fourier_constants():
    n = 256
    freq = np.arange(129)
    angle = 2 * np.pi * np.outer(np.arange(n), freq) / n
    cos, sin = np.cos(angle), np.sin(angle)
    weight = np.full(129, 2.0 / n)
    weight[[0, 128]] = 1.0 / n
    lags = np.arange(128)
    twice = np.where(lags == 0, 1.0, 2.0)
    from_power = weight[:, None] * cos[lags].T * twice
    real = (from_power @ cos[lags]) * weight
    imag = -(from_power @ sin[lags]) * weight
    to_weights = np.concatenate([real[:, :128], real[:, 128:], imag[:, 1:128]], axis=1)
    inverse = np.concatenate([weight[:, None] * cos.T, -weight[:, None] * sin.T], axis=0)
    packed = np.concatenate([cos[:, :128], cos[:, 128:], -sin[:, 1:128]], axis=1).T
    near = packed * (np.arange(n) < 129)
    factors = np.concatenate([near, packed], axis=0)
    high = factors.astype(np.float32).astype(jnp.bfloat16)
    low = (factors - high.astype(np.float64)).astype(np.float32).astype(jnp.bfloat16)
    both = np.concatenate([high, low], axis=0)
    forward = np.concatenate([cos, -sin], axis=1).astype(np.float32)
    return forward, to_weights.astype(np.float32), inverse.astype(np.float32), both


FORWARD, TO_WEIGHTS, INVERSE, FACTORS = fourier_constants()


def lag_weights_kernel(rows, middle_ref, out_ref):
    middle = middle_ref[...]
    lane = lax.broadcasted_iota(jnp.int32, middle.shape, 1)
    row = lax.broadcasted_iota(jnp.int32, (128, 128), 0)
    col = lax.broadcasted_iota(jnp.int32, (128, 128), 1)

    def one(d, turned):
        further = pltpu.roll(turned, 127, 1)
        partner = jnp.where(lane <= PERIOD - d, turned, further)
        product = (middle * partner).astype(BF16)
        keep = (row > col) & ((row <= PERIOD - d) == (col < PERIOD - d))
        sums = jnp.dot(product, keep.astype(F32).astype(BF16), preferred_element_type=F32)
        scale = jnp.where(d == 0, 1.0, 2.0).astype(F32)
        out_ref[:, pl.ds(pl.multiple_of(d * 128, 128), 128)] = (sums * scale).astype(BF16)
        return further

    lax.fori_loop(0, 64, one, middle)


def lag_weights(middle):
    rows = middle.shape[0]
    return pl.pallas_call(
        partial(lag_weights_kernel, rows),
        out_shape=jax.ShapeDtypeStruct((rows, 64 * 128), BF16),
        in_specs=[pl.BlockSpec(memory_space=pltpu.VMEM)],
        out_specs=pl.BlockSpec(memory_space=pltpu.VMEM),
        compiler_params=pltpu.CompilerParams(vmem_limit_bytes=40 * 2**20),
        name="lag_weights",
    )(middle)


def coupling_kernel(
    par_dev,
    bounds_ref,
    lag_ref,
    freq_ref,
    edge_ref,
    edge_sum_ref,
    own_ref,
    own_level_ref,
    rows_ref,
    mu_ref,
    other_ref,
    other_level_ref,
    factor_ref,
    out_ref,
    result,
    near,
    far,
    near_turn,
    far_turn,
    change,
):
    result[...] = jnp.zeros_like(result)
    padded = result.shape[1]

    def block(step, carry):
        band = lax.rem(step, BANDS)
        first = pl.multiple_of((step // BANDS) * TILE, TILE)
        columns = rows_ref[band, pl.ds(first, TILE), :].astype(F32).T
        narrow = columns.astype(BF16)
        near[0:PERIOD] = columns[0:PERIOD]
        near[PERIOD : PERIOD + 64] = columns[0:64]
        far[0:PERIOD] = columns[129:256]
        far[PERIOD : PERIOD + 64] = columns[129:193]
        for r in range(16):
            near_turn[r] = near[r : r + 176].astype(BF16)
            far_turn[r] = far[r : r + 176].astype(BF16)
        for d in range(64):
            a, r = divmod(d, 16)
            change[d * 128 : (d + 1) * 128] = (
                far_turn[0, 0:128] * far_turn[r, 16 * a : 16 * a + 128]
                - near_turn[0, 0:128] * near_turn[r, 16 * a : 16 * a + 128]
            )
        total = jnp.dot(lag_ref[band], change[...], preferred_element_type=F32)
        spectra = jnp.dot(factor_ref[0:512], narrow, preferred_element_type=F32) + jnp.dot(
            factor_ref[512:1024], narrow, preferred_element_type=F32
        )
        low_a, high_a, low_c, high_c = (spectra[128 * k : 128 * (k + 1)] for k in range(4))
        at_zero = lax.broadcasted_iota(jnp.int32, (128, TILE), 0) == 0
        cross = high_a * high_c
        real = low_a * low_c + jnp.where(at_zero, 0.0, cross)
        imag = jnp.where(at_zero, cross, low_a * high_c - high_a * low_c)
        both = jnp.concatenate([real, imag], axis=0)
        big = both.astype(BF16)
        small = (both - big.astype(F32)).astype(BF16)
        weights = freq_ref[band]
        total += jnp.dot(weights[:, 0:256], big, preferred_element_type=F32)
        total += jnp.dot(weights[:, 256:512], big, preferred_element_type=F32)
        total += jnp.dot(weights[:, 0:256], small, preferred_element_type=F32)
        mixed = jnp.dot(edge_ref[band], narrow, preferred_element_type=F32)
        mu = mu_ref[band, :, pl.ds(first, TILE)]
        total += mu * (mu * edge_sum_ref[band] - 2.0 * mixed)
        same = own_level_ref[...] == other_level_ref[:, pl.ds(first, TILE)]
        scaled = total * own_ref[band] * other_ref[band, :, pl.ds(first, TILE)]
        result[band, :, pl.ds(first, TILE)] = jnp.where(same, scaled, 0.0)
        return carry

    lax.fori_loop(bounds_ref[0] * BANDS, bounds_ref[1] * BANDS, block, 0)
    split = P1 + P2
    width = out_ref.shape[2]
    for band in range(BANDS):
        out_ref[band, :, 0:split] = result[band, 0:par_dev, 0:split]
        out_ref[band, :, split:width] = result[band, 0:par_dev, GROUP : GROUP + width - split]


def coupling_call(par_dev, total_par, bounds, *operands):
    padded, width = operands[0].shape[1], operands[6].shape[1]
    return pl.pallas_call(
        partial(coupling_kernel, par_dev),
        out_shape=jax.ShapeDtypeStruct((BANDS, par_dev, total_par), F32),
        in_specs=[pl.BlockSpec(memory_space=pltpu.SMEM)]
        + [pl.BlockSpec(memory_space=pltpu.VMEM)] * len(operands),
        out_specs=pl.BlockSpec(memory_space=pltpu.VMEM),
        scratch_shapes=[
            pltpu.VMEM((BANDS, padded, width), F32),
            pltpu.VMEM((192, TILE), F32),
            pltpu.VMEM((192, TILE), F32),
            pltpu.VMEM((16, 176, TILE), BF16),
            pltpu.VMEM((16, 176, TILE), BF16),
            pltpu.VMEM((64 * 128, TILE), BF16),
        ],
        compiler_params=pltpu.CompilerParams(vmem_limit_bytes=56 * 2**20),
        name="coupling",
    )(bounds, *operands)


def grouped(cells, axis):
    split, total = P1 + P2, cells.shape[axis]
    end = GROUP + (total - split + TILE - 1) // TILE * TILE
    pads = lambda n: [(0, n if k == axis else 0) for k in range(cells.ndim)]
    return jnp.concatenate(
        [
            jnp.pad(lax.slice_in_dim(cells, 0, split, axis=axis), pads(GROUP - split)),
            jnp.pad(
                lax.slice_in_dim(cells, split, total, axis=axis), pads(end - GROUP - total + split)
            ),
        ],
        axis=axis,
    )


def coupling_of(gathered, own_centered, owner_start, t_dev):
    total_par, par_dev = gathered.shape[0], own_centered.shape[0]
    padded = (par_dev + 15) // 16 * 16
    window, windows = lax.axis_index("tm"), lax.axis_size("tm")
    place = lax.iota(jnp.int32, t_dev + 2 * LAG)
    outside = ((window == 0) & (place < LAG)) | ((window == windows - 1) & (place >= LAG + t_dev))

    def scales(cells):
        middle = cells[:, :, LAG : LAG + t_dev].astype(F32)
        spread = lax.rsqrt(jnp.mean(middle * middle, axis=2) + EPSILON)
        power = jnp.exp2(jnp.floor(jnp.log2(spread)))
        rest = spread / power
        return power, rest * rest

    power, rest = scales(gathered)
    mu = jnp.where(window == 0, -gathered[:, :, 0].astype(F32), 0.0)
    mu = jnp.where(window == windows - 1, -gathered[:, :, -1].astype(F32), mu) * power
    inner = jnp.where(outside, 0.0, gathered.astype(F32)) * power[:, :, None]
    rows = grouped(inner.astype(BF16).transpose(1, 0, 2), 1)
    other_mu = grouped(mu.T[:, None, :], 2)
    other = grouped(rest.T[:, None, :], 2)
    other_level = grouped(resolution_of(lax.iota(jnp.int32, total_par))[None, :] - 3, 1) + 3

    own_power, own_rest = scales(own_centered)
    middle = own_centered[:, :, LAG : LAG + t_dev].astype(F32) * own_power[:, :, None]
    middle = jnp.pad(middle.transpose(1, 0, 2), ((0, 0), (0, padded - par_dev), (0, 0)))
    own = jnp.pad(own_rest.T / (t_dev * t_dev * NLAG), ((0, 0), (0, padded - par_dev)))[:, :, None]
    own_level = resolution_of(owner_start + lax.iota(jnp.int32, padded))
    own_level = jnp.where(own_level < 3, own_level, -1)[:, None]

    flat = middle.reshape(BANDS * padded, t_dev)
    lag = lag_weights(flat).reshape(BANDS, padded, 64 * 128)
    spectrum = jnp.dot(flat, FORWARD[:t_dev], precision=HIGH)
    power_spectrum = spectrum[:, :129] ** 2 + spectrum[:, 129:] ** 2
    weights = jnp.dot(power_spectrum, TO_WEIGHTS, precision=HIGH).reshape(BANDS, padded, 256)
    big = weights.astype(BF16)
    freq = jnp.concatenate([big, (weights - big.astype(F32)).astype(BF16)], axis=2)
    step = lax.iota(jnp.int32, t_dev)[:, None] + lax.iota(jnp.int32, NLAG)[None, :]
    sums = jnp.dot(flat, jnp.take(outside, step).astype(F32), precision=HIGH)
    edge_sum = jnp.sum(sums * sums, axis=1).reshape(BANDS, padded, 1)
    sums_spectrum = jnp.dot(sums, FORWARD[:NLAG], precision=HIGH)
    (a, b), (c, d) = ((x[:, :129], x[:, 129:]) for x in (sums_spectrum, spectrum))
    turned = jnp.concatenate([a * c - b * d, a * d + b * c], axis=1)
    edge = jnp.dot(turned, INVERSE, precision=HIGH).astype(BF16).reshape(BANDS, padded, 256)

    level_first = resolution_of(owner_start)
    level_last = resolution_of(jnp.minimum(owner_start + par_dev, P1 + P2 + P3) - 1)
    end = rows.shape[1] // TILE
    lo = jnp.where(level_first < 2, 0, GROUP // TILE)
    hi = jnp.where(level_last < 2, GROUP // TILE, end)
    bounds = jnp.stack([lo, hi]).astype(jnp.int32)
    return coupling_call(
        par_dev, total_par, bounds, lag, freq, edge, edge_sum, own, own_level,
        rows, other_mu, other, other_level, jnp.asarray(FACTORS),
    )


def local(source, band_taps, smooth_taps, parcel_ids):
    vert_dev, t_dev = source.shape
    owners = lax.axis_size("vert")
    total_par = (P1 + P2 + P3 + owners - 1) // owners * owners
    par_dev = total_par // owners
    n_mid = t_dev + 2 * HALF
    n_in = t_dev + 4 * HALF
    first_rows = jax.vmap(partial(toeplitz_band, n_out=n_mid, n_in=n_in))(
        band_taps.reshape(2 * BANDS, TAPS)
    )
    first_mat = first_rows.transpose(2, 0, 1).reshape(n_in, 2 * BANDS * n_mid)
    second_rows = jax.vmap(partial(toeplitz_band, n_out=t_dev, n_in=n_mid))(smooth_taps)
    second_mat = second_rows.transpose(0, 2, 1)
    widened = extended_2(source, (("tm", 1),), 2 * HALF)
    block_rows = math.gcd(vert_dev, 128)

    def filter_block(block):
        wave = jnp.dot(block, first_mat, preferred_element_type=jnp.float32).reshape(
            block_rows, 2, BANDS, n_mid
        )
        power = (wave[:, 0] * wave[:, 0] + wave[:, 1] * wave[:, 1]).astype(jnp.bfloat16)
        return jnp.einsum(
            "vbu,but->vbt", power, second_mat, preferred_element_type=jnp.float32
        ).astype(jnp.bfloat16)

    envelope = lax.map(filter_block, widened.reshape(vert_dev // block_rows, block_rows, n_in))
    flat_env = envelope.reshape(vert_dev, BANDS * t_dev)
    offsets = jnp.array([0, P1, P1 + P2], dtype=jnp.int32)
    global_ids = parcel_ids + offsets[:, None]
    owner_start = lax.axis_index("vert") * par_dev

    def one_block(block_idx):
        wanted = block_idx * par_dev + lax.iota(jnp.int32, par_dev)
        hits = jnp.sum(
            (global_ids[:, None, :] == wanted[None, :, None]).astype(jnp.bfloat16), axis=0
        )
        return jnp.dot(hits, flat_env, preferred_element_type=jnp.float32)

    pooled = lax.map(
        one_block, jnp.arange(par_dev * lax.axis_size("vert") // par_dev, dtype=jnp.int32)
    )
    own_sums = lax.psum_scatter(
        pooled.reshape(par_dev * lax.axis_size("vert"), BANDS * t_dev),
        "vert",
        scatter_dimension=0,
        tiled=True,
    )
    own_env = own_sums.reshape(par_dev, BANDS, t_dev)
    own_ext = extended_2(own_env, (("tm", 2),), LAG)
    centered, own_middle, own_spread = centered_rows(own_ext, t_dev)
    gathered = lax.all_gather(centered, "vert", axis=0, tiled=True)
    coupling = coupling_of(gathered, centered, owner_start, t_dev)
    return coupling[None]


def solution(mesh):
    return jax.shard_map(
        local,
        mesh=mesh,
        in_specs=(P("vert", "tm"), P(), P(), P(None, "vert")),
        out_specs=P("tm", None, "vert", None),
        check_vma=False,
    )
```

```python
from functools import partial

import numpy as np

import jax
import jax.numpy as jnp
from jax import lax
from jax.experimental import pallas as pl
from jax.experimental.pallas import tpu as pltpu
from jax.sharding import PartitionSpec as P

P1 = 100
P2 = 400
P3 = 1000
BANDS = 2
TAPS = 65
HALF = 32
LAG = 64
NLAG = 129
EPSILON = 1e-05
SPLIT = P1 + P2
GROUP = (SPLIT + 127) // 128 * 128
TILE = 256
PERIOD = 127
HIGH = lax.Precision.HIGHEST
BF16 = jnp.bfloat16
F32 = jnp.float32
VMEM = pl.BlockSpec(memory_space=pltpu.VMEM)


def fourier_constants():
    n = 256
    freq = np.arange(129)
    angle = 2 * np.pi * np.outer(np.arange(n), freq) / n
    cos, sin = np.cos(angle), np.sin(angle)
    weight = np.full(129, 2.0 / n)
    weight[[0, 128]] = 1.0 / n
    packed = np.concatenate([cos[:, :128], cos[:, 128:], -sin[:, 1:128]], axis=1)
    lags = np.arange(128)
    twice = np.where(lags == 0, 1.0, 2.0)
    from_power = weight[:, None] * cos[lags].T * twice
    scale = np.concatenate([weight[:128], weight[128:], weight[1:128]])
    to_weights = np.zeros((n, n))
    to_weights[:129] = (from_power @ packed[lags]) * scale
    order = np.concatenate([np.arange(64, 192), np.arange(0, 64), np.arange(192, 256)])
    inverse = (packed * scale).T[:, order]
    forward = packed * (np.arange(n) < NLAG)[:, None]
    near = forward.T[:, order]
    factors = np.concatenate([near, packed.T[:, order]], axis=0)
    high = factors.astype(np.float32).astype(jnp.bfloat16)
    low = (factors - high.astype(np.float64)).astype(np.float32).astype(jnp.bfloat16)
    f32 = lambda cells: cells.astype(np.float32)
    return f32(forward), f32(to_weights), f32(inverse), np.concatenate([high, low], axis=0)


FORWARD, TO_WEIGHTS, INVERSE, FACTORS = fourier_constants()


def params(mib):
    return pltpu.CompilerParams(vmem_limit_bytes=mib * 2**20)


def cost(flops, moved):
    return pl.CostEstimate(flops=flops, bytes_accessed=moved, transcendentals=0)


def iota(shape, dim):
    return lax.broadcasted_iota(jnp.int32, shape, dim)


class Rows:
    def __init__(self, par_dev):
        self.rows = par_dev
        self.padded = (par_dev + 15) // 16 * 16
        self.extra = (par_dev + 63) // 64
        self.height = (par_dev + 2 * self.extra + 15) // 16 * 16
        self.tail = par_dev // 16 * 16


def level_of(parcel):
    first = (parcel >= P1).astype(jnp.int32)
    second = (parcel >= SPLIT).astype(jnp.int32)
    third = (parcel >= SPLIT + P3).astype(jnp.int32)
    return first + second + third


def put_tail(form, tail, above, mean_rows):
    tail[...] = jnp.zeros_like(tail)
    tail[0 : form.rows - form.tail] = above
    high = mean_rows.astype(BF16).astype(F32)
    at = form.rows - form.tail
    tail[at : at + form.extra] = high
    tail[at + form.extra : at + 2 * form.extra] = mean_rows - high
    return tail[...].astype(BF16)


def front_kernel(
    form, owners, orders, middle_ref, left_ref, right_ref, taps_ref, smooth_ref, ids_ref, *rest
):
    outs, (env, tail) = rest[: 2 * BANDS], rest[2 * BANDS :]
    me = lax.axis_index("vert")
    shape = (256, 256)
    filters = [
        pltpu.roll(jnp.broadcast_to(taps_ref[k], shape), 192, 1, stride=1, stride_axis=0).astype(BF16)
        for k in range(2 * BANDS)
    ]
    smooths = [
        pltpu.roll(
            jnp.broadcast_to(smooth_ref[k], (128, 256)), 0, 1, stride=1, stride_axis=0
        ).astype(BF16)
        for k in range(BANDS)
    ]
    turned = (((1,), (1,)), ((), ()))
    vertices = middle_ref.shape[0]
    step = 256
    for at in range(0, vertices, step):
        cut = slice(at, at + step)
        wide = jnp.concatenate([middle_ref[cut], right_ref[cut], left_ref[cut]], axis=1)
        for band in range(BANDS):
            one = lax.dot_general(wide, filters[band], turned, preferred_element_type=F32)
            two = lax.dot_general(wide, filters[BANDS + band], turned, preferred_element_type=F32)
            power = (one * one + two * two).astype(BF16)
            smooth = lax.dot_general(power, smooths[band], turned, preferred_element_type=F32)
            env[cut, band * 128 : (band + 1) * 128] = smooth.astype(BF16)
    offsets = (0, P1, SPLIT)
    ids = [ids_ref[r : r + 1] + offsets[r] for r in range(3)]
    height = form.padded
    lane = iota((64, 128), 1)
    row = iota((64, 128), 0)
    diagonal = lax.rem(lane, 64) == row
    for k in range(owners):
        owner = me ^ k
        wanted = iota((height, 1), 0) + owner * form.rows
        hits = (wanted == ids[0]) | (wanted == ids[1]) | (wanted == ids[2])
        hits = jnp.where(hits, 1.0, 0.0).astype(BF16)
        sums = jnp.dot(hits, env[...], preferred_element_type=F32)
        for band in range(BANDS):
            cells = sums[:, band * 128 : (band + 1) * 128]
            mean = jnp.mean(cells, axis=1, keepdims=True)
            change = cells - mean
            means = jnp.concatenate(
                [
                    jnp.sum(
                        jnp.where(
                            diagonal[: min(64, height - 64 * e)], mean[64 * e : 64 * e + 64], 0.0
                        ),
                        axis=0,
                        keepdims=True,
                    )
                    for e in range(form.extra)
                ],
                axis=0,
            )
            p = place(k, orders[band][::-1])
            half = owners // 2
            out = outs[2 * band + p // half]
            out[p % half, 0 : form.tail] = change[0 : form.tail].astype(BF16)
            out[p % half, form.tail : form.height] = put_tail(
                form, tail, change[form.tail : form.rows], means
            )


def place(k, order):
    return sum((1 if k & bit else 0) << j for j, bit in enumerate(order))


def front(form, owners, orders, middle, left, right, taps, smooths, ids):
    shape = jax.ShapeDtypeStruct((owners // 2, form.height, 128), BF16)
    operands = (middle, left, right, taps, smooths, ids)
    return pl.pallas_call(
        partial(front_kernel, form, owners, orders),
        out_shape=[shape] * (2 * BANDS),
        in_specs=[VMEM] * len(operands),
        out_specs=[VMEM] * (2 * BANDS),
        scratch_shapes=[
            pltpu.VMEM((middle.shape[0], BANDS * 128), BF16),
            pltpu.VMEM((form.height - form.tail, 128), F32),
        ],
        compiler_params=params(40),
        cost_estimate=cost(3 * 10**9, 2 * 10**6),
        name="envelope_sums",
    )(*operands)


def merge_kernel(form, halves, count, *refs):
    ins, outs, tail = refs[: 2 * count], refs[2 * count : -1], refs[-1]
    blocks = ins[0].shape[0]
    at = form.rows - form.tail
    for pair in range(count):
        for n in range(blocks):
            whole = ins[2 * pair][n].astype(F32) + ins[2 * pair + 1][n].astype(F32)
            if halves == "own":
                put = outs[0].at[n]
            elif halves == "joined":
                put = outs[n].at[pair]
            else:
                put = outs[n // (blocks // 2)].at[n % (blocks // 2)]
            put[0 : form.tail] = whole[0 : form.tail].astype(BF16)
            tail[...] = whole[form.tail :]
            means = tail[at : at + form.extra] + tail[at + form.extra : at + 2 * form.extra]
            put[form.tail :] = put_tail(form, tail, whole[form.tail : form.rows], means)


def merge(form, pairs, halves):
    operands = [cells for pair in pairs for cells in pair]
    blocks = operands[0].shape[0]
    size = (form.height, 128)
    if halves == "own":
        shapes = [(blocks, *size)]
    elif halves == "joined":
        shapes = [(len(pairs), *size)] * 2
    else:
        shapes = [(blocks // 2, *size)] * 2
    return pl.pallas_call(
        partial(merge_kernel, form, halves, len(pairs)),
        out_shape=[jax.ShapeDtypeStruct(shape, BF16) for shape in shapes],
        in_specs=[VMEM] * len(operands),
        out_specs=[VMEM] * len(shapes),
        scratch_shapes=[pltpu.VMEM((form.height - form.tail, 128), F32)],
        cost_estimate=cost(10**6, 10**6),
        name="add_arrived",
    )(*operands)


def scales_of(middle):
    spread = lax.rsqrt(jnp.mean(middle * middle, axis=1, keepdims=True) + EPSILON)
    power = jnp.exp2(jnp.floor(jnp.log2(spread)))
    rest = spread / power
    return power, rest * rest


def own_rows(form, own_ref, band):
    middle = own_ref[band, 0 : form.padded].astype(F32)
    middle = jnp.where(iota(middle.shape, 0) < form.rows, middle, 0.0)
    power, rest = scales_of(middle)
    return middle * power, rest


def lag_sums_kernel(form, own_ref, out_ref):
    middle = jnp.concatenate([own_rows(form, own_ref, band)[0] for band in range(BANDS)], axis=0)
    lane = iota((1, 128), 1)
    row = iota((128, 128), 0)
    col = iota((128, 128), 1)

    def several(step, turned):
        for k in range(8):
            d = step * 8 + k
            further = pltpu.roll(turned, 127, 1)
            partner = jnp.where(lane <= PERIOD - d, turned, further)
            product = (middle * partner).astype(BF16)
            keep = (row > col) & ((row <= PERIOD - d) == (col < PERIOD - d))
            scale = jnp.where(d == 0, 1.0, 2.0).astype(F32)
            keep = jnp.where(keep, scale, 0.0).astype(BF16)
            sums = jnp.dot(product, keep, preferred_element_type=F32).astype(BF16)
            put = pl.ds(pl.multiple_of(d * 128, 128), 128)
            for band in range(BANDS):
                out_ref[band, :, put] = sums[band * form.padded : (band + 1) * form.padded]
            turned = further
        return turned

    lax.fori_loop(0, 8, several, middle)


def lag_sums(form, own):
    return pl.pallas_call(
        partial(lag_sums_kernel, form),
        out_shape=jax.ShapeDtypeStruct((BANDS, form.padded, 64 * 128), BF16),
        in_specs=[VMEM],
        out_specs=VMEM,
        compiler_params=params(40),
        cost_estimate=cost(5 * 10**9, 6 * 10**6),
        name="lag_sums",
    )(own)


def spectra_kernel(form, own_ref, forward_ref, to_weights_ref, inverse_ref, freq_ref, edge_ref, column_ref):
    window, windows = lax.axis_index("tm"), lax.axis_size("tm")
    rows = [own_rows(form, own_ref, band) for band in range(BANDS)]
    middle = jnp.concatenate([cells for cells, _ in rows], axis=0)
    rest = jnp.concatenate([left for _, left in rows], axis=0)
    dot = partial(jnp.dot, precision=HIGH, preferred_element_type=F32)
    forward = forward_ref[...]
    spectrum = dot(middle, forward_ref[0:128])
    low, high = spectrum[:, :128], spectrum[:, 128:]
    lane = iota(low.shape, 1)
    inner = jnp.where(lane == 0, 0.0, high)
    last = jnp.where(lane == 0, high, 0.0)
    strength = jnp.concatenate([low * low + inner * inner, last * last], axis=1)
    weights = dot(strength, to_weights_ref[...])
    place_in = iota((128, 256), 0) + iota((128, 256), 1)
    count = iota((128, 256), 1)
    outside = ((window == 0) & (place_in < LAG)) | (
        (window == windows - 1) & (place_in >= LAG + 128) & (count < NLAG)
    )
    outside = jnp.where(outside, 1.0, 0.0).astype(BF16)
    sums = jnp.dot(middle.astype(BF16), outside, preferred_element_type=F32)
    edge_sum = jnp.sum(sums * sums, axis=1, keepdims=True)
    other = dot(sums, forward)
    other_low, other_high = other[:, :128], other[:, 128:]
    cross = other_high * high
    real = other_low * low - jnp.where(lane == 0, 0.0, cross)
    imag = jnp.where(lane == 0, cross, other_low * high + other_high * low)
    edge = dot(jnp.concatenate([real, imag], axis=1), inverse_ref[...])
    factor = rest * (1.0 / (128 * 128 * NLAG))
    column = jnp.where(lane == 0, edge_sum, jnp.where(lane == 1, factor, 0.0))
    for band in range(BANDS):
        cut = slice(band * form.padded, (band + 1) * form.padded)
        big = weights[cut].astype(BF16)
        freq_ref[band, :, 0:256] = big
        freq_ref[band, :, 256:512] = (weights[cut] - big.astype(F32)).astype(BF16)
        edge_ref[band] = edge[cut].astype(BF16)
        column_ref[band] = column[cut]


def spectra(form, own):
    shapes = [((BANDS, form.padded, 512), BF16), ((BANDS, form.padded, 256), BF16), ((BANDS, form.padded, 128), F32)]
    return pl.pallas_call(
        partial(spectra_kernel, form),
        out_shape=[jax.ShapeDtypeStruct(*shape) for shape in shapes],
        in_specs=[VMEM] * 4,
        out_specs=[VMEM] * 3,
        compiler_params=params(40),
        cost_estimate=cost(2 * 10**9, 2 * 10**6),
        name="row_spectra",
    )(own, jnp.asarray(FORWARD), jnp.asarray(TO_WEIGHTS), jnp.asarray(INVERSE))


def mean_column(form, block):
    shape = (form.padded, form.height - form.tail)
    row, col = iota(shape, 0), iota(shape, 1) - (form.rows - form.tail)
    pick = (col == row // 64) | (col - form.extra == row // 64)
    pick = jnp.where(pick, 1.0, 0.0).astype(BF16)
    spread = jnp.dot(pick, block[form.tail :], preferred_element_type=F32)
    own = iota(spread.shape, 1) == lax.rem(iota(spread.shape, 0), 64)
    return jnp.sum(jnp.where(own, spread, 0.0), axis=1, keepdims=True)


def coupling_kernel(
    form, owners, order, band, final, lag_ref, freq_ref, edge_ref, column_ref, near_half, far_half,
    left_ref, right_ref, factor_ref, *rest
):
    if final:
        before_ref, out_ref, *scratch = rest
        result = scratch.pop(0)
    else:
        result, *scratch = rest
    blocks, rows, near, far, near_turn, far_turn, change = scratch
    me = lax.axis_index("vert")
    window, windows = lax.axis_index("tm"), lax.axis_size("tm")
    half = owners // 2
    blocks[0:half] = near_half[...]
    blocks[half:owners] = far_half[...]
    result[...] = jnp.zeros_like(result)
    rows[...] = jnp.zeros_like(rows)
    lane = iota((1, 128), 1)
    is_left = lane < LAG
    first_window, last_window = window == 0, window == windows - 1
    outside = (first_window & is_left) | (last_window & ~is_left)
    for owner in range(owners):
        k = me ^ owner
        p = sum(lax.rem(k // bit, 2) << j for j, bit in enumerate(order))
        block = blocks[p]
        middle = block[0 : form.padded].astype(F32)
        mean = mean_column(form, block)
        left, right = left_ref[p], right_ref[p]
        margins = jnp.concatenate([left, right], axis=1)
        around = margins[0 : form.padded].astype(F32)
        shift_left = mean_column(form, left) - mean
        shift_right = mean_column(form, right) - mean
        around = (around + jnp.where(is_left, shift_left, shift_right)).astype(BF16).astype(F32)
        around = jnp.where(outside, 0.0, around)
        power, left_over = scales_of(middle)
        mu = jnp.where(first_window | last_window, mean.astype(BF16).astype(F32) * power, 0.0)
        extra = jnp.where(lane == 0, mu, jnp.where(lane == 1, left_over, 0.0))
        begin = owner * form.rows
        for lo, hi, gap in ((0, SPLIT, 0), (SPLIT, owners * form.rows, GROUP - SPLIT)):
            start, stop = max(lo, begin), min(hi, begin + form.rows)
            if start < stop:
                cut = slice(start - begin, stop - begin)
                put = slice(start + gap, stop + gap)
                rows[put, 0:128] = (middle * power)[cut]
                rows[put, 128:256] = (around * power)[cut]
                rows[put, 256:384] = extra[cut]

    own_parcel = iota((form.padded, 1), 0) + me * form.rows
    own_level = level_of(own_parcel)
    own_level = jnp.where(own_level < 3, own_level, -1)
    factors = column_ref[band]
    edge_sum, own_factor = factors[:, 0:1], factors[:, 1:2]

    def tile(n, carry):
        first = pl.multiple_of(n * TILE, TILE)
        columns = rows[pl.ds(first, TILE), :].T
        narrow = columns[0:256].astype(BF16)
        near[0:64] = columns[128:192]
        near[64:127] = columns[0:63]
        near[127:191] = columns[128:192]
        far[0:63] = columns[65:128]
        far[63:127] = columns[192:256]
        far[127:190] = columns[65:128]
        far[190:191] = columns[192:193]
        for r in range(16):
            near_turn[r] = near[r : r + 176].astype(BF16)
            far_turn[r] = far[r : r + 176].astype(BF16)
        for d in range(64):
            a, r = divmod(d, 16)
            change[d * 128 : (d + 1) * 128] = (
                far_turn[0, 0:128] * far_turn[r, 16 * a : 16 * a + 128]
                - near_turn[0, 0:128] * near_turn[r, 16 * a : 16 * a + 128]
            )
        total = jnp.dot(lag_ref[band], change[...], preferred_element_type=F32)
        spectra = jnp.dot(factor_ref[0:512], narrow, preferred_element_type=F32) + jnp.dot(
            factor_ref[512:1024], narrow, preferred_element_type=F32
        )
        low_a, high_a, low_c, high_c = (spectra[128 * k : 128 * (k + 1)] for k in range(4))
        at_zero = iota((128, TILE), 0) == 0
        cross = high_a * high_c
        real = low_a * low_c + jnp.where(at_zero, 0.0, cross)
        imag = jnp.where(at_zero, cross, low_a * high_c - high_a * low_c)
        both = jnp.concatenate([real, imag], axis=0)
        big = both.astype(BF16)
        small = (both - big.astype(F32)).astype(BF16)
        weights = freq_ref[band]
        total += jnp.dot(weights[:, 0:256], big, preferred_element_type=F32)
        total += jnp.dot(weights[:, 256:512], big, preferred_element_type=F32)
        total += jnp.dot(weights[:, 0:256], small, preferred_element_type=F32)
        mixed = jnp.dot(edge_ref[band], narrow, preferred_element_type=F32)
        mu, other_factor = columns[256:257], columns[257:258]
        total += mu * (mu * edge_sum - 2.0 * mixed)
        column = iota((1, TILE), 1) + first
        parcel = jnp.where(column < GROUP, column, column - (GROUP - SPLIT))
        gap = (column >= SPLIT) & (column < GROUP)
        other_level = jnp.where(gap, 3, level_of(parcel))
        scaled = total * own_factor * other_factor
        result[:, pl.ds(first, TILE)] = jnp.where(own_level == other_level, scaled, 0.0)
        return carry

    begin = me * form.rows
    end = jnp.minimum(begin + form.rows, SPLIT + P3)
    tiles = result.shape[1] // TILE
    lax.fori_loop(
        jnp.where(begin < SPLIT, 0, GROUP // TILE),
        jnp.where(end <= SPLIT, GROUP // TILE, tiles),
        tile,
        0,
    )
    if final:
        total = owners * form.rows
        for k, cells in ((1 - band, before_ref), (band, result)):
            out_ref[:, k, 0:SPLIT] = cells[0 : form.rows, 0:SPLIT]
            out_ref[:, k, SPLIT:total] = cells[0 : form.rows, GROUP : GROUP + total - SPLIT]


def coupling(form, owners, order, band, before, *operands):
    total = owners * form.rows
    width = GROUP + (total - SPLIT + TILE - 1) // TILE * TILE
    final = before is not None
    operands = (*operands, jnp.asarray(FACTORS), *((before,) if final else ()))
    result = (form.padded, width)
    out = (form.rows, BANDS, total) if final else result
    return pl.pallas_call(
        partial(coupling_kernel, form, owners, order, band, final),
        out_shape=jax.ShapeDtypeStruct(out, F32),
        in_specs=[VMEM] * len(operands),
        out_specs=VMEM,
        scratch_shapes=([pltpu.VMEM(result, F32)] if final else [])
        + [
            pltpu.VMEM((owners, form.height, 128), BF16),
            pltpu.VMEM((width, 384), F32),
            pltpu.VMEM((192, TILE), F32),
            pltpu.VMEM((192, TILE), F32),
            pltpu.VMEM((16, 176, TILE), BF16),
            pltpu.VMEM((16, 176, TILE), BF16),
            pltpu.VMEM((64 * 128, TILE), BF16),
        ],
        compiler_params=params(56),
        cost_estimate=cost(8 * 10**9, 10**7),
        name="coupling",
    )(*operands)


def swap(cells, owners, bit):
    return lax.ppermute(cells, "vert", [(i, i ^ bit) for i in range(owners)])


def local(source, band_taps, smooth_taps, parcel_ids):
    vert_dev, t_dev = source.shape
    owners, windows = lax.axis_size("vert"), lax.axis_size("tm")
    form = Rows((P1 + P2 + P3 + owners - 1) // owners)
    bits = [1 << k for k in range(owners.bit_length() - 1)]
    orders = [bits, [bits[1], bits[0], *bits[2:]]]
    up = [(i, i + 1) for i in range(windows - 1)]
    down = [(i + 1, i) for i in range(windows - 1)]
    left = lax.ppermute(source[:, t_dev - 2 * HALF :], "tm", up)
    right = lax.ppermute(source[:, : 2 * HALF], "tm", down)
    taps = jnp.pad(band_taps.astype(F32).reshape(2 * BANDS, 1, TAPS), ((0, 0), (0, 0), (0, 256 - TAPS)))
    smooths = jnp.pad(smooth_taps.astype(F32)[:, None, :], ((0, 0), (0, 0), (0, 256 - TAPS)))
    parts = front(form, owners, orders, source, left, right, taps, smooths, parcel_ids)
    parts = [parts[0:2], parts[2:4]]
    for step in range(len(bits) - 1):
        arrived = [swap(parts[b][1], owners, orders[b][step]) for b in range(BANDS)]
        pairs = [(parts[b][0], arrived[b]) for b in range(BANDS)]
        if step < len(bits) - 2:
            parts = [merge(form, [pair], "halves") for pair in pairs]
        else:
            kept, sent = merge(form, pairs, "joined")
    arrived = swap(sent, owners, bits[-1])
    (own,) = merge(form, [(kept, arrived)], "own")

    lag = lag_sums(form, own)
    freq, edge, column = spectra(form, own)
    arrived = swap(own, owners, bits[-1])
    held = [jnp.stack([own[b], arrived[b]]) for b in range(BANDS)]
    halves = [None, None]
    for step in range(len(bits) - 2, -1, -1):
        arrived = [swap(held[b], owners, orders[b][step]) for b in range(BANDS)]
        halves = [(held[b], arrived[b]) for b in range(BANDS)]
        if step:
            held = [jnp.concatenate(pair, axis=0) for pair in halves]
    done = None
    for b in range(BANDS):
        whole = jnp.concatenate(halves[b], axis=0)
        left = lax.ppermute(whole[:, :, t_dev - LAG :], "tm", up)
        right = lax.ppermute(whole[:, :, :LAG], "tm", down)
        done = coupling(form, owners, orders[b][::-1], b, done, lag, freq, edge, column, *halves[b], left, right)
    return done.transpose(1, 0, 2)[None]


def solution(mesh):
    return jax.shard_map(
        local,
        mesh=mesh,
        in_specs=(P("vert", "tm"), P(), P(), P(None, "vert")),
        out_specs=P("tm", None, "vert", None),
        check_vma=False,
    )
```

```python
from functools import partial

import numpy as np

import jax
import jax.numpy as jnp
from jax import lax
from jax.experimental import pallas as pl
from jax.experimental.pallas import tpu as pltpu
from jax.sharding import PartitionSpec as P

P1 = 100
P2 = 400
P3 = 1000
BANDS = 2
TAPS = 65
HALF = 32
LAG = 64
NLAG = 129
EPSILON = 1e-05
SPLIT = P1 + P2
GROUP = (SPLIT + 127) // 128 * 128
TILE = 256
PERIOD = 127
HIGH = lax.Precision.HIGHEST
BF16 = jnp.bfloat16
F32 = jnp.float32
VMEM = pl.BlockSpec(memory_space=pltpu.VMEM)


def fourier_constants():
    n = 256
    freq = np.arange(129)
    angle = 2 * np.pi * np.outer(np.arange(n), freq) / n
    cos, sin = np.cos(angle), np.sin(angle)
    weight = np.full(129, 2.0 / n)
    weight[[0, 128]] = 1.0 / n
    packed = np.concatenate([cos[:, :128], cos[:, 128:], -sin[:, 1:128]], axis=1)
    lags = np.arange(128)
    twice = np.where(lags == 0, 1.0, 2.0)
    from_power = weight[:, None] * cos[lags].T * twice
    scale = np.concatenate([weight[:128], weight[128:], weight[1:128]])
    to_weights = np.zeros((n, n))
    to_weights[:129] = (from_power @ packed[lags]) * scale
    order = np.concatenate([np.arange(64, 192), np.arange(0, 64), np.arange(192, 256)])
    inverse = (packed * scale).T[:, order]
    forward = packed * (np.arange(n) < NLAG)[:, None]
    near = forward.T[:, order]
    factors = np.concatenate([near, packed.T[:, order]], axis=0)
    high = factors.astype(np.float32).astype(jnp.bfloat16)
    low = (factors - high.astype(np.float64)).astype(np.float32).astype(jnp.bfloat16)
    f32 = lambda cells: cells.astype(np.float32)
    return f32(forward), f32(to_weights), f32(inverse), np.concatenate([high, low], axis=0)


FORWARD, TO_WEIGHTS, INVERSE, FACTORS = fourier_constants()


def params(mib):
    return pltpu.CompilerParams(vmem_limit_bytes=mib * 2**20)


def cost(flops, moved):
    return pl.CostEstimate(flops=flops, bytes_accessed=moved, transcendentals=0)


def iota(shape, dim):
    return lax.broadcasted_iota(jnp.int32, shape, dim)


class Rows:
    def __init__(self, par_dev):
        self.rows = par_dev
        self.padded = (par_dev + 15) // 16 * 16
        self.extra = (par_dev + 63) // 64
        self.tail = par_dev // 16 * 16
        self.first = par_dev - self.tail
        self.height = self.tail + 32
        assert 0 < self.first <= 16 - self.extra


def level_of(parcel):
    first = (parcel >= P1).astype(jnp.int32)
    second = (parcel >= SPLIT).astype(jnp.int32)
    third = (parcel >= SPLIT + P3).astype(jnp.int32)
    return first + second + third


def put_tail(form, tail, above, mean_rows):
    tail[...] = jnp.zeros_like(tail)
    tail[0 : form.first] = above
    high = mean_rows.astype(BF16).astype(F32)
    at = form.first
    tail[at : at + form.extra] = high
    tail[at + 16 : at + 16 + form.extra] = mean_rows - high
    return tail[...].astype(BF16)


def front_kernel(
    form, owners, orders, middle_ref, first_ref, second_ref, taps_ref, smooth_ref, ids_ref, *rest
):
    outs, (env, tail) = rest[: 2 * BANDS], rest[2 * BANDS :]
    me = lax.axis_index("vert")
    shape = (256, 256)
    filters = [
        pltpu.roll(jnp.broadcast_to(taps_ref[k], shape), 192, 1, stride=1, stride_axis=0).astype(BF16)
        for k in range(2 * BANDS)
    ]
    smooths = [
        pltpu.roll(
            jnp.broadcast_to(smooth_ref[k], (128, 256)), 0, 1, stride=1, stride_axis=0
        ).astype(BF16)
        for k in range(BANDS)
    ]
    turned = (((1,), (1,)), ((), ()))
    vertices = middle_ref.shape[0]
    step = 256
    odd = lax.rem(lax.axis_index("tm"), 2) == 1
    for at in range(0, vertices, step):
        cut = slice(at, at + step)
        first, second = first_ref[cut], second_ref[cut]
        right = jnp.where(odd, second, first)[:, 0:64]
        left = jnp.where(odd, first, second)[:, 64:128]
        wide = jnp.concatenate([middle_ref[cut], right, left], axis=1)
        for band in range(BANDS):
            one = lax.dot_general(wide, filters[band], turned, preferred_element_type=F32)
            two = lax.dot_general(wide, filters[BANDS + band], turned, preferred_element_type=F32)
            power = (one * one + two * two).astype(BF16)
            smooth = lax.dot_general(power, smooths[band], turned, preferred_element_type=F32)
            env[cut, band * 128 : (band + 1) * 128] = smooth.astype(BF16)
    offsets = (0, P1, SPLIT)
    ids = [ids_ref[r : r + 1] + offsets[r] for r in range(3)]
    height = form.padded
    lane = iota((64, 128), 1)
    row = iota((64, 128), 0)
    diagonal = lax.rem(lane, 64) == row
    for k in range(owners):
        owner = me ^ k
        wanted = iota((height, 1), 0) + owner * form.rows
        hits = (wanted == ids[0]) | (wanted == ids[1]) | (wanted == ids[2])
        hits = jnp.where(hits, 1.0, 0.0).astype(BF16)
        sums = jnp.dot(hits, env[...], preferred_element_type=F32)
        for band in range(BANDS):
            cells = sums[:, band * 128 : (band + 1) * 128]
            mean = jnp.mean(cells, axis=1, keepdims=True)
            change = cells - mean
            means = jnp.concatenate(
                [
                    jnp.sum(
                        jnp.where(
                            diagonal[: min(64, height - 64 * e)], mean[64 * e : 64 * e + 64], 0.0
                        ),
                        axis=0,
                        keepdims=True,
                    )
                    for e in range(form.extra)
                ],
                axis=0,
            )
            p = place(k, orders[band][::-1])
            half = owners // 2
            out = outs[2 * band + p // half]
            out[p % half, 0 : form.tail] = change[0 : form.tail].astype(BF16)
            out[p % half, form.tail : form.height] = put_tail(
                form, tail, change[form.tail : form.rows], means
            )


def place(k, order):
    return sum((1 if k & bit else 0) << j for j, bit in enumerate(order))


def front(form, owners, orders, middle, first, second, taps, smooths, ids):
    shape = jax.ShapeDtypeStruct((owners // 2, form.height, 128), BF16)
    operands = (middle, first, second, taps, smooths, ids)
    return pl.pallas_call(
        partial(front_kernel, form, owners, orders),
        out_shape=[shape] * (2 * BANDS),
        in_specs=[VMEM] * len(operands),
        out_specs=[VMEM] * (2 * BANDS),
        scratch_shapes=[
            pltpu.VMEM((middle.shape[0], BANDS * 128), BF16),
            pltpu.VMEM((form.height - form.tail, 128), F32),
        ],
        compiler_params=params(16),
        cost_estimate=cost(3 * 10**9, 2 * 10**6),
        name="envelope_sums",
    )(*operands)


def added(form, kept, arrived):
    whole = kept.astype(F32) + arrived.astype(F32)
    high, low = whole[:, form.tail : form.tail + 16], whole[:, form.tail + 16 :]
    row = lax.broadcasted_iota(jnp.int32, high.shape, 1)
    holds = (row >= form.first) & (row < form.first + form.extra)
    mean = high + low
    big = lax.reduce_precision(mean, 8, 7)
    parts = [whole[:, : form.tail], jnp.where(holds, big, high), jnp.where(holds, mean - big, 0.0)]
    return jnp.concatenate([part.astype(BF16) for part in parts], axis=1)


def scales_of(middle):
    spread = lax.rsqrt(jnp.mean(middle * middle, axis=1, keepdims=True) + EPSILON)
    power = jnp.exp2(jnp.floor(jnp.log2(spread)))
    rest = spread / power
    return power, rest * rest


def own_rows(form, own_ref, band):
    middle = own_ref[band, 0 : form.padded].astype(F32)
    middle = jnp.where(iota(middle.shape, 0) < form.rows, middle, 0.0)
    power, rest = scales_of(middle)
    return middle * power, rest


def lag_sums_kernel(form, own_ref, out_ref):
    middle = jnp.concatenate([own_rows(form, own_ref, band)[0] for band in range(BANDS)], axis=0)
    lane = iota((1, 128), 1)
    row = iota((128, 128), 0)
    col = iota((128, 128), 1)

    def several(step, turned):
        for k in range(8):
            d = step * 8 + k
            further = pltpu.roll(turned, 127, 1)
            partner = jnp.where(lane <= PERIOD - d, turned, further)
            product = (middle * partner).astype(BF16)
            keep = (row > col) & ((row <= PERIOD - d) == (col < PERIOD - d))
            scale = jnp.where(d == 0, 1.0, 2.0).astype(F32)
            keep = jnp.where(keep, scale, 0.0).astype(BF16)
            sums = jnp.dot(product, keep, preferred_element_type=F32).astype(BF16)
            put = pl.ds(pl.multiple_of(d * 128, 128), 128)
            for band in range(BANDS):
                out_ref[band, :, put] = sums[band * form.padded : (band + 1) * form.padded]
            turned = further
        return turned

    lax.fori_loop(0, 8, several, middle)


def lag_sums(form, own):
    return pl.pallas_call(
        partial(lag_sums_kernel, form),
        out_shape=jax.ShapeDtypeStruct((BANDS, form.padded, 64 * 128), BF16),
        in_specs=[VMEM],
        out_specs=VMEM,
        compiler_params=params(12),
        cost_estimate=cost(5 * 10**9, 6 * 10**6),
        name="lag_sums",
    )(own)


def spectra_kernel(form, own_ref, forward_ref, to_weights_ref, inverse_ref, freq_ref, edge_ref, column_ref):
    window, windows = lax.axis_index("tm"), lax.axis_size("tm")
    rows = [own_rows(form, own_ref, band) for band in range(BANDS)]
    middle = jnp.concatenate([cells for cells, _ in rows], axis=0)
    rest = jnp.concatenate([left for _, left in rows], axis=0)
    dot = partial(jnp.dot, precision=HIGH, preferred_element_type=F32)
    forward = forward_ref[...]
    spectrum = dot(middle, forward_ref[0:128])
    low, high = spectrum[:, :128], spectrum[:, 128:]
    lane = iota(low.shape, 1)
    inner = jnp.where(lane == 0, 0.0, high)
    last = jnp.where(lane == 0, high, 0.0)
    strength = jnp.concatenate([low * low + inner * inner, last * last], axis=1)
    weights = dot(strength, to_weights_ref[...])
    place_in = iota((128, 256), 0) + iota((128, 256), 1)
    count = iota((128, 256), 1)
    outside = ((window == 0) & (place_in < LAG)) | (
        (window == windows - 1) & (place_in >= LAG + 128) & (count < NLAG)
    )
    outside = jnp.where(outside, 1.0, 0.0).astype(BF16)
    sums = jnp.dot(middle.astype(BF16), outside, preferred_element_type=F32)
    edge_sum = jnp.sum(sums * sums, axis=1, keepdims=True)
    other = dot(sums, forward)
    other_low, other_high = other[:, :128], other[:, 128:]
    cross = other_high * high
    real = other_low * low - jnp.where(lane == 0, 0.0, cross)
    imag = jnp.where(lane == 0, cross, other_low * high + other_high * low)
    edge = dot(jnp.concatenate([real, imag], axis=1), inverse_ref[...])
    factor = rest * (1.0 / (128 * 128 * NLAG))
    column = jnp.where(lane == 0, edge_sum, jnp.where(lane == 1, factor, 0.0))
    for band in range(BANDS):
        cut = slice(band * form.padded, (band + 1) * form.padded)
        big = weights[cut].astype(BF16)
        freq_ref[band, :, 0:256] = big
        freq_ref[band, :, 256:512] = (weights[cut] - big.astype(F32)).astype(BF16)
        edge_ref[band] = edge[cut].astype(BF16)
        column_ref[band] = column[cut]


def spectra(form, own):
    shapes = [((BANDS, form.padded, 512), BF16), ((BANDS, form.padded, 256), BF16), ((BANDS, form.padded, 128), F32)]
    return pl.pallas_call(
        partial(spectra_kernel, form),
        out_shape=[jax.ShapeDtypeStruct(*shape) for shape in shapes],
        in_specs=[VMEM] * 4,
        out_specs=[VMEM] * 3,
        compiler_params=params(12),
        cost_estimate=cost(2 * 10**9, 2 * 10**6),
        name="row_spectra",
    )(own, jnp.asarray(FORWARD), jnp.asarray(TO_WEIGHTS), jnp.asarray(INVERSE))


def mean_column(form, block):
    shape = (form.padded, form.height - form.tail)
    row, col = iota(shape, 0), iota(shape, 1) - form.first
    pick = (col == row // 64) | (col - 16 == row // 64)
    pick = jnp.where(pick, 1.0, 0.0).astype(BF16)
    spread = jnp.dot(pick, block[form.tail :], preferred_element_type=F32)
    own = iota(spread.shape, 1) == lax.rem(iota(spread.shape, 0), 64)
    return jnp.sum(jnp.where(own, spread, 0.0), axis=1, keepdims=True)


def coupling_kernel(
    form, owners, orders, lag_ref, freq_ref, edge_ref, column_ref, near_0, far_0, near_1, far_1,
    first_ref, second_ref, factor_ref, out_ref, result, blocks, rows, near, far, near_turn, far_turn, change
):
    me = lax.axis_index("vert")
    window, windows = lax.axis_index("tm"), lax.axis_size("tm")
    odd = lax.rem(window, 2) == 1
    half = owners // 2
    for band, (low, high) in enumerate(((near_0, far_0), (near_1, far_1))):
        blocks[band, 0:half] = low[...]
        blocks[band, half:owners] = high[...]
    result[...] = jnp.zeros_like(result)
    gaps = ((SPLIT, GROUP), (GROUP + owners * form.rows - SPLIT, rows.shape[1]))
    for start, stop in gaps:
        rows[:, start:stop] = jnp.zeros((BANDS, stop - start, 384), F32)
    lane = iota((1, 128), 1)
    is_left = lane < LAG
    first_window, last_window = window == 0, window == windows - 1
    outside = (first_window & is_left) | (last_window & ~is_left)
    for band in range(BANDS):
        for owner in range(owners):
            k = me ^ owner
            p = sum(lax.rem(k // bit, 2) << j for j, bit in enumerate(orders[band]))
            block = blocks[band, p]
            middle = block[0 : form.padded].astype(F32)
            mean = mean_column(form, block)
            one, two = first_ref[band, p], second_ref[band, p]
            left, right = jnp.where(odd, one, two), jnp.where(odd, two, one)
            margins = jnp.concatenate([left, right], axis=1)
            around = margins[0 : form.padded].astype(F32)
            shift_left = mean_column(form, left) - mean
            shift_right = mean_column(form, right) - mean
            around = (around + jnp.where(is_left, shift_left, shift_right)).astype(BF16).astype(F32)
            around = jnp.where(outside, 0.0, around)
            power, left_over = scales_of(middle)
            mu = jnp.where(first_window | last_window, mean.astype(BF16).astype(F32) * power, 0.0)
            extra = jnp.where(lane == 0, mu, jnp.where(lane == 1, left_over, 0.0))
            begin = owner * form.rows
            for lo, hi, gap in ((0, SPLIT, 0), (SPLIT, owners * form.rows, GROUP - SPLIT)):
                start, stop = max(lo, begin), min(hi, begin + form.rows)
                if start < stop:
                    cut = slice(start - begin, stop - begin)
                    put = slice(start + gap, stop + gap)
                    rows[band, put, 0:128] = (middle * power)[cut]
                    rows[band, put, 128:256] = (around * power)[cut]
                    rows[band, put, 256:384] = extra[cut]

    own_parcel = iota((form.padded, 1), 0) + me * form.rows
    own_level = level_of(own_parcel)
    own_level = jnp.where(own_level < 3, own_level, -1)

    def tile(step, carry):
        band = lax.rem(step, BANDS)
        first = pl.multiple_of((step // BANDS) * TILE, TILE)
        columns = rows[band, pl.ds(first, TILE), :].T
        narrow = columns[0:256].astype(BF16)
        near[0:64] = columns[128:192]
        near[64:127] = columns[0:63]
        near[127:191] = columns[128:192]
        far[0:63] = columns[65:128]
        far[63:127] = columns[192:256]
        far[127:190] = columns[65:128]
        far[190:191] = columns[192:193]
        for r in range(16):
            near_turn[r] = near[r : r + 176].astype(BF16)
            far_turn[r] = far[r : r + 176].astype(BF16)
        for d in range(64):
            a, r = divmod(d, 16)
            change[d * 128 : (d + 1) * 128] = (
                far_turn[0, 0:128] * far_turn[r, 16 * a : 16 * a + 128]
                - near_turn[0, 0:128] * near_turn[r, 16 * a : 16 * a + 128]
            )
        total = jnp.dot(lag_ref[band], change[...], preferred_element_type=F32)
        spectra = jnp.dot(factor_ref[0:512], narrow, preferred_element_type=F32) + jnp.dot(
            factor_ref[512:1024], narrow, preferred_element_type=F32
        )
        low_a, high_a, low_c, high_c = (spectra[128 * k : 128 * (k + 1)] for k in range(4))
        at_zero = iota((128, TILE), 0) == 0
        cross = high_a * high_c
        real = low_a * low_c + jnp.where(at_zero, 0.0, cross)
        imag = jnp.where(at_zero, cross, low_a * high_c - high_a * low_c)
        both = jnp.concatenate([real, imag], axis=0)
        big = both.astype(BF16)
        small = (both - big.astype(F32)).astype(BF16)
        weights = freq_ref[band]
        total += jnp.dot(weights[:, 0:256], big, preferred_element_type=F32)
        total += jnp.dot(weights[:, 256:512], big, preferred_element_type=F32)
        total += jnp.dot(weights[:, 0:256], small, preferred_element_type=F32)
        mixed = jnp.dot(edge_ref[band], narrow, preferred_element_type=F32)
        mu, other_factor = columns[256:257], columns[257:258]
        factors = column_ref[band]
        edge_sum, own_factor = factors[:, 0:1], factors[:, 1:2]
        total += mu * (mu * edge_sum - 2.0 * mixed)
        column = iota((1, TILE), 1) + first
        parcel = jnp.where(column < GROUP, column, column - (GROUP - SPLIT))
        gap = (column >= SPLIT) & (column < GROUP)
        other_level = jnp.where(gap, 3, level_of(parcel))
        scaled = total * own_factor * other_factor
        result[band, :, pl.ds(first, TILE)] = jnp.where(own_level == other_level, scaled, 0.0)
        return carry

    begin = me * form.rows
    end = jnp.minimum(begin + form.rows, SPLIT + P3)
    tiles = result.shape[2] // TILE
    lax.fori_loop(
        jnp.where(begin < SPLIT, 0, GROUP // TILE) * BANDS,
        jnp.where(end <= SPLIT, GROUP // TILE, tiles) * BANDS,
        tile,
        0,
    )
    total = owners * form.rows
    for band in range(BANDS):
        out_ref[:, band, 0:SPLIT] = result[band, 0 : form.rows, 0:SPLIT]
        out_ref[:, band, SPLIT:total] = result[band, 0 : form.rows, GROUP : GROUP + total - SPLIT]


def coupling(form, owners, orders, *operands):
    total = owners * form.rows
    width = GROUP + (total - SPLIT + TILE - 1) // TILE * TILE
    operands = (*operands, jnp.asarray(FACTORS))
    return pl.pallas_call(
        partial(coupling_kernel, form, owners, orders),
        out_shape=jax.ShapeDtypeStruct((form.rows, BANDS, total), F32),
        in_specs=[VMEM] * len(operands),
        out_specs=VMEM,
        scratch_shapes=[
            pltpu.VMEM((BANDS, form.padded, width), F32),
            pltpu.VMEM((BANDS, owners, form.height, 128), BF16),
            pltpu.VMEM((BANDS, width, 384), F32),
            pltpu.VMEM((192, TILE), F32),
            pltpu.VMEM((192, TILE), F32),
            pltpu.VMEM((16, 176, TILE), BF16),
            pltpu.VMEM((16, 176, TILE), BF16),
            pltpu.VMEM((64 * 128, TILE), BF16),
        ],
        compiler_params=params(40),
        cost_estimate=cost(16 * 10**9, 10**7),
        name="coupling",
    )(*operands)


def swap(cells, owners, bit):
    return lax.ppermute(cells, "vert", [(i, i ^ bit) for i in range(owners)])


def local(source, band_taps, smooth_taps, parcel_ids):
    vert_dev, t_dev = source.shape
    owners, windows = lax.axis_size("vert"), lax.axis_size("tm")
    form = Rows((P1 + P2 + P3 + owners - 1) // owners)
    bits = [1 << k for k in range(owners.bit_length() - 1)]
    orders = [bits, [bits[1], bits[0], *bits[2:]]]
    window = lax.axis_index("tm")
    odd = lax.rem(window, 2) == 1
    meet = [[p for i in range(k, windows - 1, 2) for p in ((i, i + 1), (i + 1, i))] for k in range(2)]
    first, second = (lax.ppermute(source, "tm", pairs) for pairs in meet)
    taps = jnp.pad(band_taps.astype(F32).reshape(2 * BANDS, 1, TAPS), ((0, 0), (0, 0), (0, 256 - TAPS)))
    smooths = jnp.pad(smooth_taps.astype(F32)[:, None, :], ((0, 0), (0, 0), (0, 256 - TAPS)))
    parts = front(form, owners, orders, source, first, second, taps, smooths, parcel_ids)
    parts = [parts[0:2], parts[2:4]]
    for step in range(len(bits) - 1):
        arrived = [swap(parts[b][1], owners, orders[b][step]) for b in range(BANDS)]
        sums = [added(form, parts[b][0], arrived[b]) for b in range(BANDS)]
        half = sums[0].shape[0] // 2
        parts = [(cells[:half], cells[half:]) for cells in sums]
    kept, sent = (jnp.concatenate([parts[b][k] for b in range(BANDS)], axis=0) for k in range(2))
    own = added(form, kept, swap(sent, owners, bits[-1]))

    lag = lag_sums(form, own)
    freq, edge, column = spectra(form, own)
    arrived = swap(own, owners, bits[-1])
    held = [jnp.stack([own[b], arrived[b]]) for b in range(BANDS)]
    halves = [None, None]
    for step in range(len(bits) - 2, -1, -1):
        arrived = [swap(held[b], owners, orders[b][step]) for b in range(BANDS)]
        halves = [(held[b], arrived[b]) for b in range(BANDS)]
        if step:
            held = [jnp.concatenate(pair, axis=0) for pair in halves]
    whole = jnp.stack([jnp.concatenate(pair, axis=0) for pair in halves])
    early, late = whole[..., :LAG], whole[..., t_dev - LAG :]
    first = lax.ppermute(jnp.where(odd, early, late), "tm", meet[0])
    second = lax.ppermute(jnp.where(odd, late, early), "tm", meet[1])
    turned = [order[::-1] for order in orders]
    done = coupling(form, owners, turned, lag, freq, edge, column, *halves[0], *halves[1], first, second)
    return done.transpose(1, 0, 2)[None]


def solution(mesh):
    return jax.shard_map(
        local,
        mesh=mesh,
        in_specs=(P("vert", "tm"), P(), P(), P(None, "vert")),
        out_specs=P("tm", None, "vert", None),
        check_vma=False,
    )
```

```python
from functools import partial

import numpy as np

import jax
import jax.numpy as jnp
from jax import lax
from jax.experimental import pallas as pl
from jax.experimental.pallas import tpu as pltpu
from jax.sharding import PartitionSpec as P

P1 = 100
P2 = 400
P3 = 1000
BANDS = 2
TAPS = 65
HALF = 32
LAG = 64
NLAG = 129
EPSILON = 1e-05
SPLIT = P1 + P2
GROUP = (SPLIT + 127) // 128 * 128
TILE = 256
PERIOD = 127
HIGH = lax.Precision.HIGHEST
BF16 = jnp.bfloat16
F32 = jnp.float32
VMEM = pl.BlockSpec(memory_space=pltpu.VMEM)


def fourier_constants():
    n = 256
    freq = np.arange(129)
    angle = 2 * np.pi * np.outer(np.arange(n), freq) / n
    cos, sin = np.cos(angle), np.sin(angle)
    weight = np.full(129, 2.0 / n)
    weight[[0, 128]] = 1.0 / n
    packed = np.concatenate([cos[:, :128], cos[:, 128:], -sin[:, 1:128]], axis=1)
    lags = np.arange(128)
    twice = np.where(lags == 0, 1.0, 2.0)
    from_power = weight[:, None] * cos[lags].T * twice
    scale = np.concatenate([weight[:128], weight[128:], weight[1:128]])
    to_weights = np.zeros((n, n))
    to_weights[:129] = (from_power @ packed[lags]) * scale
    order = np.concatenate([np.arange(64, 192), np.arange(0, 64), np.arange(192, 256)])
    inverse = (packed * scale).T[:, order]
    forward = packed * (np.arange(n) < NLAG)[:, None]
    near = forward.T[:, order]
    factors = np.concatenate([near, packed.T[:, order]], axis=0)
    high = factors.astype(np.float32).astype(jnp.bfloat16)
    low = (factors - high.astype(np.float64)).astype(np.float32).astype(jnp.bfloat16)
    f32 = lambda cells: cells.astype(np.float32)
    return f32(forward), f32(to_weights), f32(inverse), np.concatenate([high, low], axis=0)


FORWARD, TO_WEIGHTS, INVERSE, FACTORS = fourier_constants()


def params(mib):
    return pltpu.CompilerParams(vmem_limit_bytes=mib * 2**20)


def cost(flops, moved):
    return pl.CostEstimate(flops=flops, bytes_accessed=moved, transcendentals=0)


def iota(shape, dim):
    return lax.broadcasted_iota(jnp.int32, shape, dim)


class Rows:
    def __init__(self, par_dev):
        self.rows = par_dev
        self.padded = (par_dev + 15) // 16 * 16
        self.extra = (par_dev + 63) // 64
        self.tail = par_dev // 16 * 16
        self.first = par_dev - self.tail
        self.height = self.tail + 32
        assert 0 < self.first <= 16 - self.extra


def level_of(parcel):
    first = (parcel >= P1).astype(jnp.int32)
    second = (parcel >= SPLIT).astype(jnp.int32)
    third = (parcel >= SPLIT + P3).astype(jnp.int32)
    return first + second + third


def put_tail(form, tail, above, mean_rows):
    tail[...] = jnp.zeros_like(tail)
    tail[0 : form.first] = above
    high = mean_rows.astype(BF16).astype(F32)
    at = form.first
    tail[at : at + form.extra] = high
    tail[at + 16 : at + 16 + form.extra] = mean_rows - high
    return tail[...].astype(BF16)


def front_kernel(
    form, owners, orders, middle_ref, first_ref, second_ref, taps_ref, smooth_ref, ids_ref, *rest
):
    outs, (env, tail) = rest[: 2 * BANDS], rest[2 * BANDS :]
    me = lax.axis_index("vert")
    shape = (256, 256)
    filters = [
        pltpu.roll(jnp.broadcast_to(taps_ref[k], shape), 192, 1, stride=1, stride_axis=0).astype(BF16)
        for k in range(2 * BANDS)
    ]
    smooths = [
        pltpu.roll(
            jnp.broadcast_to(smooth_ref[k], (128, 256)), 0, 1, stride=1, stride_axis=0
        ).astype(BF16)
        for k in range(BANDS)
    ]
    turned = (((1,), (1,)), ((), ()))
    vertices = middle_ref.shape[0]
    step = 256
    odd = lax.rem(lax.axis_index("tm"), 2) == 1
    for at in range(0, vertices, step):
        cut = slice(at, at + step)
        first, second = first_ref[cut], second_ref[cut]
        right = jnp.where(odd, second, first)[:, 0:64]
        left = jnp.where(odd, first, second)[:, 64:128]
        wide = jnp.concatenate([middle_ref[cut], right, left], axis=1)
        for band in range(BANDS):
            one = lax.dot_general(wide, filters[band], turned, preferred_element_type=F32)
            two = lax.dot_general(wide, filters[BANDS + band], turned, preferred_element_type=F32)
            power = (one * one + two * two).astype(BF16)
            smooth = lax.dot_general(power, smooths[band], turned, preferred_element_type=F32)
            env[cut, band * 128 : (band + 1) * 128] = smooth.astype(BF16)
    offsets = (0, P1, SPLIT)
    ids = [ids_ref[r : r + 1] + offsets[r] for r in range(3)]
    height = form.padded
    lane = iota((64, 128), 1)
    row = iota((64, 128), 0)
    diagonal = lax.rem(lane, 64) == row
    for k in range(owners):
        owner = me ^ k
        wanted = iota((height, 1), 0) + owner * form.rows
        hits = (wanted == ids[0]) | (wanted == ids[1]) | (wanted == ids[2])
        hits = jnp.where(hits, 1.0, 0.0).astype(BF16)
        sums = jnp.dot(hits, env[...], preferred_element_type=F32)
        for band in range(BANDS):
            cells = sums[:, band * 128 : (band + 1) * 128]
            mean = jnp.mean(cells, axis=1, keepdims=True)
            change = cells - mean
            means = jnp.concatenate(
                [
                    jnp.sum(
                        jnp.where(
                            diagonal[: min(64, height - 64 * e)], mean[64 * e : 64 * e + 64], 0.0
                        ),
                        axis=0,
                        keepdims=True,
                    )
                    for e in range(form.extra)
                ],
                axis=0,
            )
            p = place(k, orders[band][::-1])
            half = owners // 2
            out = outs[2 * band + p // half]
            out[p % half, 0 : form.tail] = change[0 : form.tail].astype(BF16)
            out[p % half, form.tail : form.height] = put_tail(
                form, tail, change[form.tail : form.rows], means
            )


def place(k, order):
    return sum((1 if k & bit else 0) << j for j, bit in enumerate(order))


def front(form, owners, orders, middle, first, second, taps, smooths, ids):
    shape = jax.ShapeDtypeStruct((owners // 2, form.height, 128), BF16)
    operands = (middle, first, second, taps, smooths, ids)
    return pl.pallas_call(
        partial(front_kernel, form, owners, orders),
        out_shape=[shape] * (2 * BANDS),
        in_specs=[VMEM] * len(operands),
        out_specs=[VMEM] * (2 * BANDS),
        scratch_shapes=[
            pltpu.VMEM((middle.shape[0], BANDS * 128), BF16),
            pltpu.VMEM((form.height - form.tail, 128), F32),
        ],
        compiler_params=params(16),
        cost_estimate=cost(3 * 10**9, 2 * 10**6),
        name="envelope_sums",
    )(*operands)


def added(form, kept, arrived):
    whole = kept.astype(F32) + arrived.astype(F32)
    high, low = whole[:, form.tail : form.tail + 16], whole[:, form.tail + 16 :]
    row = lax.broadcasted_iota(jnp.int32, high.shape, 1)
    holds = (row >= form.first) & (row < form.first + form.extra)
    mean = high + low
    big = lax.reduce_precision(mean, 8, 7)
    parts = [whole[:, : form.tail], jnp.where(holds, big, high), jnp.where(holds, mean - big, 0.0)]
    return jnp.concatenate([part.astype(BF16) for part in parts], axis=1)


def scales_of(middle):
    spread = lax.rsqrt(jnp.mean(middle * middle, axis=1, keepdims=True) + EPSILON)
    power = jnp.exp2(jnp.floor(jnp.log2(spread)))
    rest = spread / power
    return power, rest * rest


def own_rows(form, own_ref, band):
    middle = own_ref[band, 0 : form.padded].astype(F32)
    middle = jnp.where(iota(middle.shape, 0) < form.rows, middle, 0.0)
    power, rest = scales_of(middle)
    return middle * power, rest


def lag_sums_kernel(form, band, own_ref, out_ref):
    middle = own_rows(form, own_ref, band)[0]
    lane = iota((1, 128), 1)
    row = iota((128, 128), 0)
    col = iota((128, 128), 1)
    turned = middle
    for d in range(64):
        further = pltpu.roll(middle, PERIOD - d, 1)
        partner = jnp.where(lane <= PERIOD - d, turned, further)
        product = (middle * partner).astype(BF16)
        keep = (row > col) & ((row <= PERIOD - d) == (col < PERIOD - d))
        keep = jnp.where(keep, 2.0 if d else 1.0, 0.0).astype(BF16)
        sums = jnp.dot(product, keep, preferred_element_type=F32)
        out_ref[:, d * 128 : (d + 1) * 128] = sums.astype(BF16)
        turned = further


def lag_sums(form, band, own):
    return pl.pallas_call(
        partial(lag_sums_kernel, form, band),
        out_shape=jax.ShapeDtypeStruct((form.padded, 64 * 128), BF16),
        in_specs=[VMEM],
        out_specs=VMEM,
        compiler_params=params(12),
        cost_estimate=cost(2 * 10**9, 3 * 10**6),
        name="lag_sums",
    )(own)


def spectra_kernel(form, own_ref, forward_ref, to_weights_ref, inverse_ref, freq_ref, edge_ref, column_ref):
    window, windows = lax.axis_index("tm"), lax.axis_size("tm")
    rows = [own_rows(form, own_ref, band) for band in range(BANDS)]
    middle = jnp.concatenate([cells for cells, _ in rows], axis=0)
    rest = jnp.concatenate([left for _, left in rows], axis=0)
    dot = partial(jnp.dot, precision=HIGH, preferred_element_type=F32)
    forward = forward_ref[...]
    spectrum = dot(middle, forward_ref[0:128])
    low, high = spectrum[:, :128], spectrum[:, 128:]
    lane = iota(low.shape, 1)
    inner = jnp.where(lane == 0, 0.0, high)
    last = jnp.where(lane == 0, high, 0.0)
    strength = jnp.concatenate([low * low + inner * inner, last * last], axis=1)
    weights = dot(strength, to_weights_ref[...])
    place_in = iota((128, 256), 0) + iota((128, 256), 1)
    count = iota((128, 256), 1)
    outside = ((window == 0) & (place_in < LAG)) | (
        (window == windows - 1) & (place_in >= LAG + 128) & (count < NLAG)
    )
    outside = jnp.where(outside, 1.0, 0.0).astype(BF16)
    sums = jnp.dot(middle.astype(BF16), outside, preferred_element_type=F32)
    edge_sum = jnp.sum(sums * sums, axis=1, keepdims=True)
    other = dot(sums, forward)
    other_low, other_high = other[:, :128], other[:, 128:]
    cross = other_high * high
    real = other_low * low - jnp.where(lane == 0, 0.0, cross)
    imag = jnp.where(lane == 0, cross, other_low * high + other_high * low)
    edge = dot(jnp.concatenate([real, imag], axis=1), inverse_ref[...])
    factor = rest * (1.0 / (128 * 128 * NLAG))
    column = jnp.where(lane == 0, edge_sum, jnp.where(lane == 1, factor, 0.0))
    for band in range(BANDS):
        cut = slice(band * form.padded, (band + 1) * form.padded)
        big = weights[cut].astype(BF16)
        freq_ref[band, :, 0:256] = big
        freq_ref[band, :, 256:512] = (weights[cut] - big.astype(F32)).astype(BF16)
        edge_ref[band] = edge[cut].astype(BF16)
        column_ref[band] = column[cut]


def spectra(form, own):
    shapes = [((BANDS, form.padded, 512), BF16), ((BANDS, form.padded, 256), BF16), ((BANDS, form.padded, 128), F32)]
    return pl.pallas_call(
        partial(spectra_kernel, form),
        out_shape=[jax.ShapeDtypeStruct(*shape) for shape in shapes],
        in_specs=[VMEM] * 4,
        out_specs=[VMEM] * 3,
        compiler_params=params(12),
        cost_estimate=cost(2 * 10**9, 2 * 10**6),
        name="row_spectra",
    )(own, jnp.asarray(FORWARD), jnp.asarray(TO_WEIGHTS), jnp.asarray(INVERSE))


def mean_column(form, block, at=0):
    shape = (form.padded, form.height - form.tail)
    row, col = iota(shape, 0), iota(shape, 1) - form.first
    pick = (col == row // 64) | (col - 16 == row // 64)
    pick = jnp.where(pick, 1.0, 0.0).astype(BF16)
    spread = jnp.dot(pick, block[form.tail :], preferred_element_type=F32)
    own = iota(spread.shape, 1) == lax.rem(iota(spread.shape, 0), 64) + at
    return jnp.sum(jnp.where(own, spread, 0.0), axis=1, keepdims=True)


def margins_kernel(form, owners, *refs):
    halves, outs = refs[: 2 * BANDS], refs[2 * BANDS :]
    odd = lax.rem(lax.axis_index("tm"), 2) == 1
    is_low = iota((1, 128), 1) < LAG
    half = owners // 2
    for n in range(owners):
        zero, one = (halves[2 * band + n // half][n % half].astype(F32) for band in range(BANDS))
        early = jnp.where(is_low, zero, pltpu.roll(one, 64, 1)).astype(BF16)
        late = jnp.where(is_low, pltpu.roll(zero, 64, 1), one).astype(BF16)
        outs[0][n] = jnp.where(odd, early, late)
        outs[1][n] = jnp.where(odd, late, early)


def margins(form, owners, *halves):
    return pl.pallas_call(
        partial(margins_kernel, form, owners),
        out_shape=[jax.ShapeDtypeStruct((owners, form.height, 128), BF16)] * 2,
        in_specs=[VMEM] * len(halves),
        out_specs=[VMEM] * 2,
        compiler_params=params(8),
        cost_estimate=cost(10**6, 2 * 10**6),
        name="margins",
    )(*halves)


def coupling_kernel(
    form, owners, orders, lag_0, lag_1, freq_ref, edge_ref, column_ref, near_0, far_0, near_1, far_1,
    first_ref, second_ref, factor_ref, out_ref, result, blocks, rows, near, far, near_turn, far_turn, change
):
    me = lax.axis_index("vert")
    window, windows = lax.axis_index("tm"), lax.axis_size("tm")
    odd = lax.rem(window, 2) == 1
    half = owners // 2
    for band, (low, high) in enumerate(((near_0, far_0), (near_1, far_1))):
        blocks[band, 0:half] = low[...]
        blocks[band, half:owners] = high[...]
    result[...] = jnp.zeros_like(result)
    gaps = ((SPLIT, GROUP), (GROUP + owners * form.rows - SPLIT, rows.shape[1]))
    for start, stop in gaps:
        rows[:, start:stop] = jnp.zeros((BANDS, stop - start, 384), F32)
    lane = iota((1, 128), 1)
    is_left = lane < LAG
    first_window, last_window = window == 0, window == windows - 1
    outside = (first_window & is_left) | (last_window & ~is_left)
    for band in range(BANDS):
        for owner in range(owners):
            k = me ^ owner
            p = sum(lax.rem(k // bit, 2) << j for j, bit in enumerate(orders[band]))
            block = blocks[band, p]
            middle = block[0 : form.padded].astype(F32)
            mean = mean_column(form, block)
            one, two = first_ref[p], second_ref[p]
            left, right = jnp.where(odd, one, two), jnp.where(odd, two, one)
            shift_left = mean_column(form, left, band * 64) - mean
            shift_right = mean_column(form, right, band * 64) - mean
            left, right = (cells[0 : form.padded].astype(F32) for cells in (left, right))
            if band == 0:
                right = pltpu.roll(right, 64, 1)
            else:
                left = pltpu.roll(left, 64, 1)
            around = jnp.where(is_left, left, right)
            around = (around + jnp.where(is_left, shift_left, shift_right)).astype(BF16).astype(F32)
            around = jnp.where(outside, 0.0, around)
            power, left_over = scales_of(middle)
            mu = jnp.where(first_window | last_window, mean.astype(BF16).astype(F32) * power, 0.0)
            extra = jnp.where(lane == 0, mu, jnp.where(lane == 1, left_over, 0.0))
            begin = owner * form.rows
            for lo, hi, gap in ((0, SPLIT, 0), (SPLIT, owners * form.rows, GROUP - SPLIT)):
                start, stop = max(lo, begin), min(hi, begin + form.rows)
                if start < stop:
                    cut = slice(start - begin, stop - begin)
                    put = slice(start + gap, stop + gap)
                    rows[band, put, 0:128] = (middle * power)[cut]
                    rows[band, put, 128:256] = (around * power)[cut]
                    rows[band, put, 256:384] = extra[cut]

    own_parcel = iota((form.padded, 1), 0) + me * form.rows
    own_level = level_of(own_parcel)
    own_level = jnp.where(own_level < 3, own_level, -1)

    def tile(band, start, height, step, carry):
        lag_ref = (lag_0, lag_1)[band]
        rows_of = slice(start, start + height)
        first = pl.multiple_of(step * TILE, TILE)
        columns = rows[band, pl.ds(first, TILE), :].T
        narrow = columns[0:256].astype(BF16)
        near[0:64] = columns[128:192]
        near[64:127] = columns[0:63]
        near[127:191] = columns[128:192]
        far[0:63] = columns[65:128]
        far[63:127] = columns[192:256]
        far[127:190] = columns[65:128]
        far[190:191] = columns[192:193]
        for r in range(16):
            near_turn[r] = near[r : r + 176].astype(BF16)
            far_turn[r] = far[r : r + 176].astype(BF16)
        for d in range(64):
            a, r = divmod(d, 16)
            change[d * 128 : (d + 1) * 128] = (
                far_turn[0, 0:128] * far_turn[r, 16 * a : 16 * a + 128]
                - near_turn[0, 0:128] * near_turn[r, 16 * a : 16 * a + 128]
            )
        total = jnp.dot(lag_ref[rows_of], change[...], preferred_element_type=F32)
        spectra = jnp.dot(factor_ref[0:512], narrow, preferred_element_type=F32) + jnp.dot(
            factor_ref[512:1024], narrow, preferred_element_type=F32
        )
        low_a, high_a, low_c, high_c = (spectra[128 * k : 128 * (k + 1)] for k in range(4))
        at_zero = iota((128, TILE), 0) == 0
        cross = high_a * high_c
        real = low_a * low_c + jnp.where(at_zero, 0.0, cross)
        imag = jnp.where(at_zero, cross, low_a * high_c - high_a * low_c)
        both = jnp.concatenate([real, imag], axis=0)
        big = both.astype(BF16)
        small = (both - big.astype(F32)).astype(BF16)
        weights = freq_ref[band, rows_of]
        total += jnp.dot(weights[:, 0:256], big, preferred_element_type=F32)
        total += jnp.dot(weights[:, 256:512], big, preferred_element_type=F32)
        total += jnp.dot(weights[:, 0:256], small, preferred_element_type=F32)
        mixed = jnp.dot(edge_ref[band, rows_of], narrow, preferred_element_type=F32)
        mu, other_factor = columns[256:257], columns[257:258]
        factors = column_ref[band, rows_of]
        edge_sum, own_factor = factors[:, 0:1], factors[:, 1:2]
        total += mu * (mu * edge_sum - 2.0 * mixed)
        column = iota((1, TILE), 1) + first
        parcel = jnp.where(column < GROUP, column, column - (GROUP - SPLIT))
        gap = (column >= SPLIT) & (column < GROUP)
        other_level = jnp.where(gap, 3, level_of(parcel))
        scaled = total * own_factor * other_factor
        same = own_level[rows_of] == other_level
        result[band, rows_of, pl.ds(first, TILE)] = jnp.where(same, scaled, 0.0)
        return carry

    begin = me * form.rows
    end = jnp.minimum(begin + form.rows, SPLIT + P3)
    tiles = result.shape[2] // TILE
    fold = GROUP // TILE
    coarse, fine = begin < SPLIT, end > SPLIT
    for band in range(BANDS):
        run = lambda lo, hi, start, height: lax.fori_loop(
            lo, hi, partial(tile, band, start, height), 0
        )
        low, high = jnp.where(coarse, 0, fold), jnp.where(fine, tiles, fold)
        cut = SPLIT % form.rows
        if form.padded - 128 <= cut <= 128:
            mixed = coarse & fine
            run(0, jnp.where(mixed, fold, 0), 0, 128)
            run(jnp.where(mixed, fold, tiles), tiles, form.padded - 128, 128)
            low = jnp.where(mixed, high, low)
        run(low, high, 0, form.padded)
    total = owners * form.rows
    for band in range(BANDS):
        out_ref[:, band, 0:SPLIT] = result[band, 0 : form.rows, 0:SPLIT]
        out_ref[:, band, SPLIT:total] = result[band, 0 : form.rows, GROUP : GROUP + total - SPLIT]


def coupling(form, owners, orders, *operands):
    total = owners * form.rows
    width = GROUP + (total - SPLIT + TILE - 1) // TILE * TILE
    operands = (*operands, jnp.asarray(FACTORS))
    return pl.pallas_call(
        partial(coupling_kernel, form, owners, orders),
        out_shape=jax.ShapeDtypeStruct((form.rows, BANDS, total), F32),
        in_specs=[VMEM] * len(operands),
        out_specs=VMEM,
        scratch_shapes=[
            pltpu.VMEM((BANDS, form.padded, width), F32),
            pltpu.VMEM((BANDS, owners, form.height, 128), BF16),
            pltpu.VMEM((BANDS, width, 384), F32),
            pltpu.VMEM((192, TILE), F32),
            pltpu.VMEM((192, TILE), F32),
            pltpu.VMEM((16, 176, TILE), BF16),
            pltpu.VMEM((16, 176, TILE), BF16),
            pltpu.VMEM((64 * 128, TILE), BF16),
        ],
        compiler_params=params(24),
        cost_estimate=cost(16 * 10**9, 10**7),
        name="coupling",
    )(*operands)


def swap(cells, owners, bit):
    return lax.ppermute(cells, "vert", [(i, i ^ bit) for i in range(owners)])


def local(source, band_taps, smooth_taps, parcel_ids):
    vert_dev, t_dev = source.shape
    owners, windows = lax.axis_size("vert"), lax.axis_size("tm")
    form = Rows((P1 + P2 + P3 + owners - 1) // owners)
    bits = [1 << k for k in range(owners.bit_length() - 1)]
    orders = [bits, [bits[1], bits[0], *bits[2:]]]
    meet = [[p for i in range(k, windows - 1, 2) for p in ((i, i + 1), (i + 1, i))] for k in range(2)]
    first, second = (lax.ppermute(source, "tm", pairs) for pairs in meet)
    taps = jnp.pad(band_taps.astype(F32).reshape(2 * BANDS, 1, TAPS), ((0, 0), (0, 0), (0, 256 - TAPS)))
    smooths = jnp.pad(smooth_taps.astype(F32)[:, None, :], ((0, 0), (0, 0), (0, 256 - TAPS)))
    parts = front(form, owners, orders, source, first, second, taps, smooths, parcel_ids)
    parts = [parts[0:2], parts[2:4]]
    for step in range(len(bits) - 1):
        arrived = [swap(parts[b][1], owners, orders[b][step]) for b in range(BANDS)]
        sums = [added(form, parts[b][0], arrived[b]) for b in range(BANDS)]
        half = sums[0].shape[0] // 2
        parts = [(cells[:half], cells[half:]) for cells in sums]
    kept, sent = (jnp.concatenate([parts[b][k] for b in range(BANDS)], axis=0) for k in range(2))
    own = added(form, kept, swap(sent, owners, bits[-1]))

    lag = [lag_sums(form, band, own) for band in range(BANDS)]
    freq, edge, column = spectra(form, own)
    arrived = swap(own, owners, bits[-1])
    held = [jnp.stack([own[b], arrived[b]]) for b in range(BANDS)]
    held, lag[0] = lax.optimization_barrier((held, lag[0]))
    halves = [None, None]
    for step in range(len(bits) - 2, -1, -1):
        arrived = [swap(held[b], owners, orders[b][step]) for b in range(BANDS)]
        halves = [(held[b], arrived[b]) for b in range(BANDS)]
        if step:
            held = [jnp.concatenate(pair, axis=0) for pair in halves]
    first, second = margins(form, owners, *halves[0], *halves[1])
    first = lax.ppermute(first, "tm", meet[0])
    second = lax.ppermute(second, "tm", meet[1])
    turned = [order[::-1] for order in orders]
    done = coupling(form, owners, turned, *lag, freq, edge, column, *halves[0], *halves[1], first, second)
    return done.transpose(1, 0, 2)[None]


def solution(mesh):
    return jax.shard_map(
        local,
        mesh=mesh,
        in_specs=(P("vert", "tm"), P(), P(), P(None, "vert")),
        out_specs=P("tm", None, "vert", None),
        check_vma=False,
    )
```

```python
from functools import partial

import numpy as np

import jax
import jax.numpy as jnp
from jax import lax
from jax.experimental import pallas as pl
from jax.experimental.pallas import tpu as pltpu
from jax.sharding import PartitionSpec as P

P1 = 100
P2 = 400
P3 = 1000
BANDS = 2
TAPS = 65
HALF = 32
LAG = 64
NLAG = 129
EPSILON = 1e-05
SPLIT = P1 + P2
GROUP = (SPLIT + 127) // 128 * 128
TILE = 256
PERIOD = 127
LAGS = 64 * 128
HIGH = lax.Precision.HIGHEST
BF16 = jnp.bfloat16
F32 = jnp.float32
VMEM = pl.BlockSpec(memory_space=pltpu.VMEM)


def fourier_constants():
    n = 256
    freq = np.arange(129)
    angle = 2 * np.pi * np.outer(np.arange(n), freq) / n
    cos, sin = np.cos(angle), np.sin(angle)
    weight = np.full(129, 2.0 / n)
    weight[[0, 128]] = 1.0 / n
    packed = np.concatenate([cos[:, :128], cos[:, 128:], -sin[:, 1:128]], axis=1)
    lags = np.arange(128)
    twice = np.where(lags == 0, 1.0, 2.0)
    from_power = weight[:, None] * cos[lags].T * twice
    scale = np.concatenate([weight[:128], weight[128:], weight[1:128]])
    to_weights = np.zeros((n, n))
    to_weights[:129] = (from_power @ packed[lags]) * scale
    order = np.concatenate([np.arange(64, 192), np.arange(0, 64), np.arange(192, 256)])
    inverse = (packed * scale).T[:, order]
    forward = packed * (np.arange(n) < NLAG)[:, None]
    near = forward.T[:, order]
    factors = np.concatenate([near, packed.T[:, order]], axis=0)
    high = factors.astype(np.float32).astype(jnp.bfloat16)
    low = (factors - high.astype(np.float64)).astype(np.float32).astype(jnp.bfloat16)
    f32 = lambda cells: cells.astype(np.float32)
    return f32(forward), f32(to_weights), f32(inverse), np.concatenate([high, low], axis=1)


FORWARD, TO_WEIGHTS, INVERSE, FACTORS = fourier_constants()


def params(mib):
    return pltpu.CompilerParams(vmem_limit_bytes=mib * 2**20)


def cost(flops, moved):
    return pl.CostEstimate(flops=flops, bytes_accessed=moved, transcendentals=0)


def iota(shape, dim):
    return lax.broadcasted_iota(jnp.int32, shape, dim)


class Rows:
    def __init__(self, par_dev):
        self.rows = par_dev
        self.padded = (par_dev + 15) // 16 * 16
        self.extra = (par_dev + 63) // 64
        self.tail = par_dev // 16 * 16
        self.first = par_dev - self.tail
        self.height = self.tail + 32
        assert 0 < self.first <= 16 - self.extra


def level_of(parcel):
    first = (parcel >= P1).astype(jnp.int32)
    second = (parcel >= SPLIT).astype(jnp.int32)
    third = (parcel >= SPLIT + P3).astype(jnp.int32)
    return first + second + third


def put_tail(form, tail, above, mean_rows):
    tail[...] = jnp.zeros_like(tail)
    tail[0 : form.first] = above
    high = mean_rows.astype(BF16).astype(F32)
    at = form.first
    tail[at : at + form.extra] = high
    tail[at + 16 : at + 16 + form.extra] = mean_rows - high
    return tail[...].astype(BF16)


def prepare_kernel(form, owners, middle_ref, taps_ref, smooth_ref, ids_ref, source_ref, filter_ref, smoother_ref, hits_ref):
    me = lax.axis_index("vert")
    source_ref[...] = middle_ref[...]
    for k in range(2 * BANDS):
        taps = jnp.broadcast_to(taps_ref[k], (256, 256))
        filter_ref[k] = pltpu.roll(taps, 192, 1, stride=1, stride_axis=0).astype(BF16)
    for k in range(BANDS):
        taps = jnp.broadcast_to(smooth_ref[k], (128, 256))
        smoother_ref[k] = pltpu.roll(taps, 0, 1, stride=1, stride_axis=0).astype(BF16)
    offsets = (0, P1, SPLIT)
    ids = [ids_ref[r : r + 1] + offsets[r] for r in range(3)]
    for k in range(owners):
        wanted = iota((form.padded, 1), 0) + (me ^ k) * form.rows
        hits = (wanted == ids[0]) | (wanted == ids[1]) | (wanted == ids[2])
        hits_ref[k] = jnp.where(hits, 1.0, 0.0).astype(BF16)


def prepare(form, owners, source, taps, smooths, ids):
    shapes = [source.shape, (2 * BANDS, 256, 256), (BANDS, 128, 256), (owners, form.padded, source.shape[0])]
    return pl.pallas_call(
        partial(prepare_kernel, form, owners),
        out_shape=[jax.ShapeDtypeStruct(shape, BF16) for shape in shapes],
        in_specs=[VMEM] * 4,
        out_specs=[VMEM] * 4,
        compiler_params=params(16),
        cost_estimate=cost(2 * 10**9, 5 * 10**6),
        name="prepare",
    )(source, taps, smooths, ids)


def front_kernel(form, owners, orders, first_ref, second_ref, middle_ref, filter_ref, smoother_ref, hits_ref, *rest):
    outs, (env, tail) = rest[: 2 * BANDS], rest[2 * BANDS :]
    filters = [filter_ref[k] for k in range(2 * BANDS)]
    smooths = [smoother_ref[k] for k in range(BANDS)]
    turned = (((1,), (1,)), ((), ()))
    vertices = middle_ref.shape[0]
    step = 256
    odd = lax.rem(lax.axis_index("tm"), 2) == 1
    for at in range(0, vertices, step):
        cut = slice(at, at + step)
        first, second = first_ref[cut], second_ref[cut]
        right = jnp.where(odd, second, first)[:, 0:64]
        left = jnp.where(odd, first, second)[:, 64:128]
        wide = jnp.concatenate([middle_ref[cut], right, left], axis=1)
        for band in range(BANDS):
            one = lax.dot_general(wide, filters[band], turned, preferred_element_type=F32)
            two = lax.dot_general(wide, filters[BANDS + band], turned, preferred_element_type=F32)
            power = (one * one + two * two).astype(BF16)
            smooth = lax.dot_general(power, smooths[band], turned, preferred_element_type=F32)
            env[cut, band * 128 : (band + 1) * 128] = smooth.astype(BF16)
    height = form.padded
    lane = iota((64, 128), 1)
    row = iota((64, 128), 0)
    diagonal = lax.rem(lane, 64) == row
    for k in range(owners):
        sums = jnp.dot(hits_ref[k], env[...], preferred_element_type=F32)
        for band in range(BANDS):
            cells = sums[:, band * 128 : (band + 1) * 128]
            mean = jnp.mean(cells, axis=1, keepdims=True)
            change = cells - mean
            means = jnp.concatenate(
                [
                    jnp.sum(
                        jnp.where(
                            diagonal[: min(64, height - 64 * e)], mean[64 * e : 64 * e + 64], 0.0
                        ),
                        axis=0,
                        keepdims=True,
                    )
                    for e in range(form.extra)
                ],
                axis=0,
            )
            p = place(k, orders[band][::-1])
            half = owners // 2
            out = outs[2 * band + p // half]
            out[p % half, 0 : form.tail] = change[0 : form.tail].astype(BF16)
            out[p % half, form.tail : form.height] = put_tail(
                form, tail, change[form.tail : form.rows], means
            )


def place(k, order):
    return sum((1 if k & bit else 0) << j for j, bit in enumerate(order))


def front(form, owners, orders, first, second, middle, *prepared):
    shape = jax.ShapeDtypeStruct((owners // 2, form.height, 128), BF16)
    operands = (first, second, middle, *prepared)
    return pl.pallas_call(
        partial(front_kernel, form, owners, orders),
        out_shape=[shape] * (2 * BANDS),
        in_specs=[VMEM] * len(operands),
        out_specs=[VMEM] * (2 * BANDS),
        scratch_shapes=[
            pltpu.VMEM((middle.shape[0], BANDS * 128), BF16),
            pltpu.VMEM((form.height - form.tail, 128), F32),
        ],
        compiler_params=params(16),
        cost_estimate=cost(3 * 10**9, 2 * 10**6),
        name="envelope_sums",
    )(*operands)


def added(form, kept, arrived):
    whole = kept.astype(F32) + arrived.astype(F32)
    high, low = whole[:, form.tail : form.tail + 16], whole[:, form.tail + 16 :]
    row = lax.broadcasted_iota(jnp.int32, high.shape, 1)
    holds = (row >= form.first) & (row < form.first + form.extra)
    mean = high + low
    big = lax.reduce_precision(mean, 8, 7)
    parts = [whole[:, : form.tail], jnp.where(holds, big, high), jnp.where(holds, mean - big, 0.0)]
    return jnp.concatenate([part.astype(BF16) for part in parts], axis=1)


def scales_of(middle):
    spread = lax.rsqrt(jnp.mean(middle * middle, axis=1, keepdims=True) + EPSILON)
    power = jnp.exp2(jnp.floor(jnp.log2(spread)))
    rest = spread / power
    return power, rest * rest


def own_rows(form, own_ref, band):
    middle = own_ref[band, 0 : form.padded].astype(F32)
    middle = jnp.where(iota(middle.shape, 0) < form.rows, middle, 0.0)
    power, rest = scales_of(middle)
    return middle * power, rest


def row_weights_kernel(form, band, own_ref, forward_ref, to_weights_ref, inverse_ref, out_ref, column_ref):
    middle, rest = own_rows(form, own_ref, band)
    lane = iota((1, 128), 1)
    row = iota((128, 128), 0)
    col = iota((128, 128), 1)
    turned = middle
    for d in range(64):
        further = pltpu.roll(middle, PERIOD - d, 1)
        partner = jnp.where(lane <= PERIOD - d, turned, further)
        product = (middle * partner).astype(BF16)
        keep = (row > col) & ((row <= PERIOD - d) == (col < PERIOD - d))
        keep = jnp.where(keep, 2.0 if d else 1.0, 0.0).astype(BF16)
        sums = jnp.dot(product, keep, preferred_element_type=F32)
        out_ref[:, d * 128 : (d + 1) * 128] = sums.astype(BF16)
        turned = further

    window, windows = lax.axis_index("tm"), lax.axis_size("tm")
    dot = partial(jnp.dot, precision=HIGH, preferred_element_type=F32)
    spectrum = dot(middle, forward_ref[0:128])
    low, high = spectrum[:, :128], spectrum[:, 128:]
    inner = jnp.where(lane == 0, 0.0, high)
    last = jnp.where(lane == 0, high, 0.0)
    strength = jnp.concatenate([low * low + inner * inner, last * last], axis=1)
    weights = dot(strength, to_weights_ref[...])
    place_in = iota((128, 256), 0) + iota((128, 256), 1)
    count = iota((128, 256), 1)
    outside = ((window == 0) & (place_in < LAG)) | (
        (window == windows - 1) & (place_in >= LAG + 128) & (count < NLAG)
    )
    outside = jnp.where(outside, 1.0, 0.0).astype(BF16)
    sums = jnp.dot(middle.astype(BF16), outside, preferred_element_type=F32)
    edge_sum = jnp.sum(sums * sums, axis=1, keepdims=True)
    other = dot(sums, forward_ref[...])
    other_low, other_high = other[:, :128], other[:, 128:]
    cross = other_high * high
    real = other_low * low - jnp.where(lane == 0, 0.0, cross)
    imag = jnp.where(lane == 0, cross, other_low * high + other_high * low)
    edge = dot(jnp.concatenate([real, imag], axis=1), inverse_ref[...])
    big = weights.astype(BF16)
    out_ref[:, LAGS : LAGS + 256] = big
    out_ref[:, LAGS + 256 : LAGS + 512] = (weights - big.astype(F32)).astype(BF16)
    out_ref[:, LAGS + 512 : LAGS + 768] = big
    out_ref[:, LAGS + 768 : LAGS + 1024] = edge.astype(BF16)
    factor = rest * (1.0 / (128 * 128 * NLAG))
    column_ref[...] = jnp.where(lane == 0, edge_sum, jnp.where(lane == 1, factor, 0.0))


def row_weights(form, band, own):
    shapes = [((form.padded, LAGS + 1024), BF16), ((form.padded, 128), F32)]
    return pl.pallas_call(
        partial(row_weights_kernel, form, band),
        out_shape=[jax.ShapeDtypeStruct(*shape) for shape in shapes],
        in_specs=[VMEM] * 4,
        out_specs=[VMEM] * 2,
        compiler_params=params(12),
        cost_estimate=cost(3 * 10**9, 4 * 10**6),
        name="row_weights",
    )(own, jnp.asarray(FORWARD), jnp.asarray(TO_WEIGHTS), jnp.asarray(INVERSE))


def mean_column(form, block, at=0):
    shape = (form.padded, form.height - form.tail)
    row, col = iota(shape, 0), iota(shape, 1) - form.first
    pick = (col == row // 64) | (col - 16 == row // 64)
    pick = jnp.where(pick, 1.0, 0.0).astype(BF16)
    spread = jnp.dot(pick, block[form.tail :], preferred_element_type=F32)
    own = iota(spread.shape, 1) == lax.rem(iota(spread.shape, 0), 64) + at
    return jnp.sum(jnp.where(own, spread, 0.0), axis=1, keepdims=True)


def pieces(form, owners, owner):
    at = owner * form.rows
    found = []
    for lo, hi, gap in ((0, SPLIT, 0), (SPLIT, owners * form.rows, GROUP - SPLIT)):
        start, stop = max(lo, at), min(hi, at + form.rows)
        if start < stop:
            found.append((slice(start - at, stop - at), slice(start + gap, stop + gap)))
    return found


def stands(order, k):
    return sum(lax.rem(k // bit, 2) << j for j, bit in enumerate(order))


def gaps(form, owners):
    end = GROUP + owners * form.rows - SPLIT
    return (slice(SPLIT, GROUP), slice(end, columns_of(form, owners)))


def columns_of(form, owners):
    return GROUP + (owners * form.rows - SPLIT + TILE - 1) // TILE * TILE


def scaled_rows_kernel(form, owners, orders, near_0, far_0, near_1, far_1, middle_ref, extra_ref, blocks):
    me = lax.axis_index("vert")
    window, windows = lax.axis_index("tm"), lax.axis_size("tm")
    edge = (window == 0) | (window == windows - 1)
    half = owners // 2
    lane = iota((1, 128), 1)
    for band, (low, high) in enumerate(((near_0, far_0), (near_1, far_1))):
        blocks[0:half] = low[...]
        blocks[half:owners] = high[...]
        for cut in gaps(form, owners):
            middle_ref[band, cut] = jnp.zeros((cut.stop - cut.start, 128), F32)
            extra_ref[band, cut] = jnp.zeros((cut.stop - cut.start, 128), F32)
        for owner in range(owners):
            block = blocks[stands(orders[band], me ^ owner)]
            middle = block[0 : form.padded].astype(F32)
            mean = mean_column(form, block)
            power, left_over = scales_of(middle)
            mu = jnp.where(edge, mean.astype(BF16).astype(F32) * power, 0.0)
            scaled = middle * power
            extra = jnp.where(lane == 0, mu, jnp.where(lane == 1, left_over, jnp.where(lane == 2, power, mean)))
            for cut, put in pieces(form, owners, owner):
                middle_ref[band, put] = scaled[cut]
                extra_ref[band, put] = extra[cut]


def scaled_rows(form, owners, orders, *halves):
    shape = jax.ShapeDtypeStruct((BANDS, columns_of(form, owners), 128), F32)
    return pl.pallas_call(
        partial(scaled_rows_kernel, form, owners, orders),
        out_shape=[shape] * 2,
        in_specs=[VMEM] * len(halves),
        out_specs=[VMEM] * 2,
        scratch_shapes=[pltpu.VMEM((owners, form.height, 128), BF16)],
        compiler_params=params(12),
        cost_estimate=cost(10**9, 4 * 10**6),
        name="scaled_rows",
    )(*halves)


def margins_kernel(owners, *refs):
    halves, outs = refs[:BANDS], refs[BANDS:]
    odd = lax.rem(lax.axis_index("tm"), 2) == 1
    is_low = iota((1, 128), 1) < LAG
    for n in range(owners):
        zero, one = (halves[band][n].astype(F32) for band in range(BANDS))
        early = jnp.where(is_low, zero, pltpu.roll(one, 64, 1)).astype(BF16)
        late = jnp.where(is_low, pltpu.roll(zero, 64, 1), one).astype(BF16)
        outs[0][n] = jnp.where(odd, early, late)
        outs[1][n] = jnp.where(odd, late, early)


def margins(*halves):
    return pl.pallas_call(
        partial(margins_kernel, halves[0].shape[0]),
        out_shape=[jax.ShapeDtypeStruct(halves[0].shape, BF16)] * 2,
        in_specs=[VMEM] * len(halves),
        out_specs=[VMEM] * 2,
        compiler_params=params(8),
        cost_estimate=cost(10**6, 2 * 10**6),
        name="margins",
    )(*halves)


def coupling_kernel(
    form, owners, orders, lag_0, lag_1, column_0, column_1, middle_ref, extra_ref,
    first_0, second_0, first_1, second_1, factor_ref, out_ref, result, first_ref, second_ref, around_rows, near, far, near_turn, far_turn, change
):
    me = lax.axis_index("vert")
    window, windows = lax.axis_index("tm"), lax.axis_size("tm")
    odd = lax.rem(window, 2) == 1
    half = owners // 2
    for whole, low, high in ((first_ref, first_0, first_1), (second_ref, second_0, second_1)):
        whole[0:half] = low[...]
        whole[half:owners] = high[...]
    result[...] = jnp.zeros_like(result)
    for cut in gaps(form, owners):
        around_rows[:, cut] = jnp.zeros((BANDS, cut.stop - cut.start, 128), F32)
    lane = iota((1, 128), 1)
    is_left = lane < LAG
    first_window, last_window = window == 0, window == windows - 1
    outside = (first_window & is_left) | (last_window & ~is_left)
    begin = me * form.rows
    end = jnp.minimum(begin + form.rows, SPLIT + P3)
    coarse, fine = begin < SPLIT, end > SPLIT
    for band in range(BANDS):
        for owner in range(owners):
            p = stands(orders[band], me ^ owner)
            one, two = first_ref[p], second_ref[p]
            left, right = jnp.where(odd, one, two), jnp.where(odd, two, one)
            shift_left = mean_column(form, left, band * 64)
            shift_right = mean_column(form, right, band * 64)
            left, right = (cells[0 : form.padded].astype(F32) for cells in (left, right))
            if band == 0:
                right = pltpu.roll(right, 64, 1)
            else:
                left = pltpu.roll(left, 64, 1)
            around = jnp.where(is_left, left + shift_left, right + shift_right)
            for cut, put in pieces(form, owners, owner):
                extra = extra_ref[band, put]
                shifted = (around[cut] - extra[:, 3:4]).astype(BF16).astype(F32) * extra[:, 2:3]
                around_rows[band, put] = jnp.where(outside, 0.0, shifted)

    own_parcel = iota((form.padded, 1), 0) + me * form.rows
    own_level = level_of(own_parcel)
    own_level = jnp.where(own_level < 3, own_level, -1)

    def tile(band, start, height, step, carry):
        lag_ref = (lag_0, lag_1)[band]
        rows_of = slice(start, start + height)
        first = pl.multiple_of(step * TILE, TILE)
        tile_of = pl.ds(first, TILE)
        columns = jnp.concatenate([middle_ref[band, tile_of].T, around_rows[band, tile_of].T], axis=0)
        constants = extra_ref[band, tile_of].T
        narrow = columns.astype(BF16)
        near[0:64] = columns[128:192]
        near[64:127] = columns[0:63]
        near[127:191] = columns[128:192]
        far[0:63] = columns[65:128]
        far[63:127] = columns[192:256]
        far[127:190] = columns[65:128]
        far[190:191] = columns[192:193]
        twice = jnp.concatenate([narrow, narrow], axis=0)
        spectra = jnp.dot(factor_ref[...], twice, preferred_element_type=F32)
        low_a, high_a, low_c, high_c = (spectra[128 * k : 128 * (k + 1)] for k in range(4))
        at_zero = iota((128, TILE), 0) == 0
        cross = high_a * high_c
        real = low_a * low_c + jnp.where(at_zero, 0.0, cross)
        imag = jnp.where(at_zero, cross, low_a * high_c - high_a * low_c)
        both = jnp.concatenate([real, imag], axis=0)
        big = both.astype(BF16)
        small = (both - big.astype(F32)).astype(BF16)
        mu, other_factor = constants[0:1], constants[1:2]
        mixed = (columns * (-2.0 * mu)).astype(BF16)
        for n, part in enumerate((big, big, small, mixed)):
            change[LAGS + 256 * n : LAGS + 256 * (n + 1)] = part
        for r in range(16):
            near_turn[r] = near[r : r + 176].astype(BF16)
            far_turn[r] = far[r : r + 176].astype(BF16)
        for d in range(64):
            a, r = divmod(d, 16)
            change[d * 128 : (d + 1) * 128] = (
                far_turn[0, 0:128] * far_turn[r, 16 * a : 16 * a + 128]
                - near_turn[0, 0:128] * near_turn[r, 16 * a : 16 * a + 128]
            )
        total = jnp.dot(lag_ref[rows_of], change[...], preferred_element_type=F32)
        factors = (column_0, column_1)[band][rows_of]
        edge_sum, own_factor = factors[:, 0:1], factors[:, 1:2]
        total += mu * mu * edge_sum
        column = iota((1, TILE), 1) + first
        parcel = jnp.where(column < GROUP, column, column - (GROUP - SPLIT))
        gap = (column >= SPLIT) & (column < GROUP)
        other_level = jnp.where(gap, 3, level_of(parcel))
        scaled = total * own_factor * other_factor
        same = own_level[rows_of] == other_level
        result[band, rows_of, pl.ds(first, TILE)] = jnp.where(same, scaled, 0.0)
        return carry

    tiles = result.shape[2] // TILE
    fold = GROUP // TILE
    for band in range(BANDS):
        run = lambda lo, hi, start, height: lax.fori_loop(
            lo, hi, partial(tile, band, start, height), 0
        )
        low, high = jnp.where(coarse, 0, fold), jnp.where(fine, tiles, fold)
        cut = SPLIT % form.rows
        if form.padded - 128 <= cut <= 128:
            mixed = coarse & fine
            run(0, jnp.where(mixed, fold, 0), 0, 128)
            run(jnp.where(mixed, fold, tiles), tiles, form.padded - 128, 128)
            low = jnp.where(mixed, high, low)
        run(low, high, 0, form.padded)
    total = owners * form.rows
    for band in range(BANDS):
        out_ref[:, band, 0:SPLIT] = result[band, 0 : form.rows, 0:SPLIT]
        out_ref[:, band, SPLIT:total] = result[band, 0 : form.rows, GROUP : GROUP + total - SPLIT]


def coupling(form, owners, orders, *operands):
    total = owners * form.rows
    width = columns_of(form, owners)
    operands = (*operands, jnp.asarray(FACTORS))
    return pl.pallas_call(
        partial(coupling_kernel, form, owners, orders),
        out_shape=jax.ShapeDtypeStruct((form.rows, BANDS, total), F32),
        in_specs=[VMEM] * len(operands),
        out_specs=VMEM,
        scratch_shapes=[
            pltpu.VMEM((BANDS, form.padded, width), F32),
            pltpu.VMEM((owners, form.height, 128), BF16),
            pltpu.VMEM((owners, form.height, 128), BF16),
            pltpu.VMEM((BANDS, width, 128), F32),
            pltpu.VMEM((192, TILE), F32),
            pltpu.VMEM((192, TILE), F32),
            pltpu.VMEM((16, 176, TILE), BF16),
            pltpu.VMEM((16, 176, TILE), BF16),
            pltpu.VMEM((LAGS + 1024, TILE), BF16),
        ],
        compiler_params=params(24),
        cost_estimate=cost(16 * 10**9, 10**7),
        name="coupling",
    )(*operands)


def swap(cells, owners, bit):
    return lax.ppermute(cells, "vert", [(i, i ^ bit) for i in range(owners)])


def local(source, band_taps, smooth_taps, parcel_ids):
    vert_dev, t_dev = source.shape
    owners, windows = lax.axis_size("vert"), lax.axis_size("tm")
    form = Rows((P1 + P2 + P3 + owners - 1) // owners)
    bits = [1 << k for k in range(owners.bit_length() - 1)]
    orders = [bits, [bits[1], bits[0], *bits[2:]]]
    meet = [[p for i in range(k, windows - 1, 2) for p in ((i, i + 1), (i + 1, i))] for k in range(2)]
    first, second = (lax.ppermute(source, "tm", pairs) for pairs in meet)
    taps = jnp.pad(band_taps.astype(F32).reshape(2 * BANDS, 1, TAPS), ((0, 0), (0, 0), (0, 256 - TAPS)))
    smooths = jnp.pad(smooth_taps.astype(F32)[:, None, :], ((0, 0), (0, 0), (0, 256 - TAPS)))
    prepared = prepare(form, owners, source, taps, smooths, parcel_ids)
    parts = front(form, owners, orders, first, second, *prepared)
    parts = [parts[0:2], parts[2:4]]
    for step in range(len(bits) - 1):
        arrived = [swap(parts[b][1], owners, orders[b][step]) for b in range(BANDS)]
        sums = [added(form, parts[b][0], arrived[b]) for b in range(BANDS)]
        half = sums[0].shape[0] // 2
        parts = [(cells[:half], cells[half:]) for cells in sums]
    kept, sent = (jnp.concatenate([parts[b][k] for b in range(BANDS)], axis=0) for k in range(2))
    theirs = swap(jnp.concatenate([kept, sent], axis=0), owners, bits[-1])
    both = added(form, jnp.concatenate([kept, sent], axis=0), jnp.concatenate([theirs[BANDS:], theirs[:BANDS]], axis=0))
    own = both[:BANDS]
    held = [jnp.stack([both[b], both[BANDS + b]]) for b in range(BANDS)]
    weights = [row_weights(form, 0, own), None]
    sides = []

    def send_margins(packed):
        sides.append([lax.ppermute(cells, "tm", pairs) for cells, pairs in zip(packed, meet)])

    for step in range(len(bits) - 2, -1, -1):
        arrived = [swap(held[b], owners, orders[b][step]) for b in range(BANDS)]
        if step:
            held = [jnp.concatenate([held[b], arrived[b]], axis=0) for b in range(BANDS)]
            if step == 1:
                held, weights[0] = lax.optimization_barrier((held, weights[0]))
        else:
            packed, own = lax.optimization_barrier((margins(*held), own))
            send_margins(packed)
            weights[1] = row_weights(form, 1, own)
            arrived, weights[1] = lax.optimization_barrier((arrived, weights[1]))
            send_margins(margins(*arrived))
    turned = [order[::-1] for order in orders]
    middle, extra = scaled_rows(form, owners, turned, held[0], arrived[0], held[1], arrived[1])
    lag, column = zip(*weights)
    done = coupling(form, owners, turned, *lag, *column, middle, extra, *sides[0], *sides[1])
    return done.transpose(1, 0, 2)[None]


def solution(mesh):
    return jax.shard_map(
        local,
        mesh=mesh,
        in_specs=(P("vert", "tm"), P(), P(), P(None, "vert")),
        out_specs=P("tm", None, "vert", None),
        check_vma=False,
    )
```

```python
from functools import partial

import numpy as np

import jax
import jax.numpy as jnp
from jax import lax
from jax.experimental import pallas as pl
from jax.experimental.pallas import tpu as pltpu
from jax.sharding import PartitionSpec as P

P1 = 100
P2 = 400
P3 = 1000
BANDS = 2
TAPS = 65
HALF = 32
LAG = 64
NLAG = 129
EPSILON = 1e-05
SPLIT = P1 + P2
GROUP = (SPLIT + 127) // 128 * 128
TILE = 256
PERIOD = 127
LAGS = 64 * 128
HIGH = lax.Precision.HIGHEST
BF16 = jnp.bfloat16
F32 = jnp.float32
VMEM = pl.BlockSpec(memory_space=pltpu.VMEM)


def fourier_constants():
    n = 256
    freq = np.arange(129)
    angle = 2 * np.pi * np.outer(np.arange(n), freq) / n
    cos, sin = np.cos(angle), np.sin(angle)
    weight = np.full(129, 2.0 / n)
    weight[[0, 128]] = 1.0 / n
    packed = np.concatenate([cos[:, :128], cos[:, 128:], -sin[:, 1:128]], axis=1)
    lags = np.arange(128)
    twice = np.where(lags == 0, 1.0, 2.0)
    from_power = weight[:, None] * cos[lags].T * twice
    scale = np.concatenate([weight[:128], weight[128:], weight[1:128]])
    to_weights = np.zeros((n, n))
    to_weights[:129] = (from_power @ packed[lags]) * scale
    order = np.concatenate([np.arange(64, 192), np.arange(0, 64), np.arange(192, 256)])
    inverse = (packed * scale).T[:, order]
    forward = packed * (np.arange(n) < NLAG)[:, None]
    near = forward.T[:, order]
    factors = np.concatenate([near, packed.T[:, order]], axis=0)
    high = factors.astype(np.float32).astype(jnp.bfloat16)
    low = (factors - high.astype(np.float64)).astype(np.float32).astype(jnp.bfloat16)
    f32 = lambda cells: cells.astype(np.float32)
    return f32(forward), f32(to_weights), f32(inverse), np.concatenate([high, low], axis=1)


FORWARD, TO_WEIGHTS, INVERSE, FACTORS = fourier_constants()


def params(mib):
    return pltpu.CompilerParams(vmem_limit_bytes=mib * 2**20)


def cost(flops, moved):
    return pl.CostEstimate(flops=flops, bytes_accessed=moved, transcendentals=0)


def iota(shape, dim):
    return lax.broadcasted_iota(jnp.int32, shape, dim)


class Rows:
    def __init__(self, par_dev):
        self.rows = par_dev
        self.padded = (par_dev + 15) // 16 * 16
        self.extra = (par_dev + 63) // 64
        self.tail = par_dev // 16 * 16
        self.first = par_dev - self.tail
        self.height = self.tail + 32
        assert 0 < self.first <= 16 - self.extra


def level_of(parcel):
    first = (parcel >= P1).astype(jnp.int32)
    second = (parcel >= SPLIT).astype(jnp.int32)
    third = (parcel >= SPLIT + P3).astype(jnp.int32)
    return first + second + third


def put_tail(form, tail, above, mean_rows):
    tail[...] = jnp.zeros_like(tail)
    tail[0 : form.first] = above
    high = mean_rows.astype(BF16).astype(F32)
    at = form.first
    tail[at : at + form.extra] = high
    tail[at + 16 : at + 16 + form.extra] = mean_rows - high
    return tail[...].astype(BF16)


def prepare_kernel(form, owners, middle_ref, taps_ref, ids_ref, source_ref, filter_ref, smoother_ref, hits_ref):
    me = lax.axis_index("vert")
    source_ref[...] = middle_ref[...]
    for k in range(2 * BANDS):
        taps = jnp.broadcast_to(taps_ref[k : k + 1], (256, 256))
        filter_ref[k] = pltpu.roll(taps, 192, 1, stride=1, stride_axis=0).astype(BF16)
    for k in range(BANDS):
        taps = jnp.broadcast_to(taps_ref[4 + k : 5 + k], (128, 256))
        smoother_ref[k] = pltpu.roll(taps, 0, 1, stride=1, stride_axis=0).astype(BF16)
    offsets = (0, P1, SPLIT)
    ids = [ids_ref[r : r + 1] + offsets[r] for r in range(3)]
    for k in range(owners):
        wanted = iota((form.padded, 1), 0) + (me ^ k) * form.rows
        hits = (wanted == ids[0]) | (wanted == ids[1]) | (wanted == ids[2])
        hits_ref[k] = jnp.where(hits, 1.0, 0.0).astype(BF16)


def prepare(form, owners, source, taps, ids):
    shapes = [source.shape, (2 * BANDS, 256, 256), (BANDS, 128, 256), (owners, form.padded, source.shape[0])]
    return pl.pallas_call(
        partial(prepare_kernel, form, owners),
        out_shape=[jax.ShapeDtypeStruct(shape, BF16) for shape in shapes],
        in_specs=[VMEM] * 3,
        out_specs=[VMEM] * 4,
        compiler_params=params(16),
        cost_estimate=cost(2 * 10**9, 5 * 10**6),
        name="prepare",
    )(source, taps, ids)


def front_kernel(form, owners, orders, first_ref, second_ref, middle_ref, filter_ref, smoother_ref, hits_ref, *rest):
    outs, (env, tail) = rest[: 2 * BANDS], rest[2 * BANDS :]
    filters = [filter_ref[k] for k in range(2 * BANDS)]
    smooths = [smoother_ref[k] for k in range(BANDS)]
    turned = (((1,), (1,)), ((), ()))
    vertices = middle_ref.shape[0]
    step = 256
    odd = lax.rem(lax.axis_index("tm"), 2) == 1
    for at in range(0, vertices, step):
        cut = slice(at, at + step)
        first, second = first_ref[cut], second_ref[cut]
        right = jnp.where(odd, second, first)[:, 0:64]
        left = jnp.where(odd, first, second)[:, 64:128]
        wide = jnp.concatenate([middle_ref[cut], right, left], axis=1)
        for band in range(BANDS):
            one = lax.dot_general(wide, filters[band], turned, preferred_element_type=F32)
            two = lax.dot_general(wide, filters[BANDS + band], turned, preferred_element_type=F32)
            power = (one * one + two * two).astype(BF16)
            smooth = lax.dot_general(power, smooths[band], turned, preferred_element_type=F32)
            env[cut, band * 128 : (band + 1) * 128] = smooth.astype(BF16)
    height = form.padded
    lane = iota((64, 128), 1)
    row = iota((64, 128), 0)
    diagonal = lax.rem(lane, 64) == row
    for k in range(owners):
        sums = jnp.dot(hits_ref[k], env[...], preferred_element_type=F32)
        for band in range(BANDS):
            cells = sums[:, band * 128 : (band + 1) * 128]
            mean = jnp.mean(cells, axis=1, keepdims=True)
            change = cells - mean
            means = jnp.concatenate(
                [
                    jnp.sum(
                        jnp.where(
                            diagonal[: min(64, height - 64 * e)], mean[64 * e : 64 * e + 64], 0.0
                        ),
                        axis=0,
                        keepdims=True,
                    )
                    for e in range(form.extra)
                ],
                axis=0,
            )
            p = place(k, orders[band][::-1])
            half = owners // 2
            out = outs[2 * band + p // half]
            out[p % half, 0 : form.tail] = change[0 : form.tail].astype(BF16)
            out[p % half, form.tail : form.height] = put_tail(
                form, tail, change[form.tail : form.rows], means
            )


def place(k, order):
    return sum((1 if k & bit else 0) << j for j, bit in enumerate(order))


def front(form, owners, orders, first, second, middle, *prepared):
    shape = jax.ShapeDtypeStruct((owners // 2, form.height, 128), BF16)
    operands = (first, second, middle, *prepared)
    return pl.pallas_call(
        partial(front_kernel, form, owners, orders),
        out_shape=[shape] * (2 * BANDS),
        in_specs=[VMEM] * len(operands),
        out_specs=[VMEM] * (2 * BANDS),
        scratch_shapes=[
            pltpu.VMEM((middle.shape[0], BANDS * 128), BF16),
            pltpu.VMEM((form.height - form.tail, 128), F32),
        ],
        compiler_params=params(16),
        cost_estimate=cost(3 * 10**9, 2 * 10**6),
        name="envelope_sums",
    )(*operands)


def added(form, kept, arrived):
    whole = kept.astype(F32) + arrived.astype(F32)
    high, low = whole[:, form.tail : form.tail + 16], whole[:, form.tail + 16 :]
    row = lax.broadcasted_iota(jnp.int32, high.shape, 1)
    holds = (row >= form.first) & (row < form.first + form.extra)
    mean = high + low
    big = lax.reduce_precision(mean, 8, 7)
    parts = [whole[:, : form.tail], jnp.where(holds, big, high), jnp.where(holds, mean - big, 0.0)]
    return jnp.concatenate([part.astype(BF16) for part in parts], axis=1)


def scales_of(middle):
    spread = lax.rsqrt(jnp.mean(middle * middle, axis=1, keepdims=True) + EPSILON)
    power = jnp.exp2(jnp.floor(jnp.log2(spread)))
    rest = spread / power
    return power, rest * rest


def own_rows(form, own_ref, band):
    middle = own_ref[band, 0 : form.padded].astype(F32)
    middle = jnp.where(iota(middle.shape, 0) < form.rows, middle, 0.0)
    power, rest = scales_of(middle)
    return middle * power, rest


def lag_sums_kernel(form, band, own_ref, out_ref):
    middle = own_rows(form, own_ref, band)[0]
    lane = iota((1, 128), 1)
    row = iota((128, 128), 0)
    col = iota((128, 128), 1)
    turned = middle
    for d in range(64):
        further = pltpu.roll(middle, PERIOD - d, 1)
        partner = jnp.where(lane <= PERIOD - d, turned, further)
        product = (middle * partner).astype(BF16)
        keep = (row > col) & ((row <= PERIOD - d) == (col < PERIOD - d))
        keep = jnp.where(keep, 2.0 if d else 1.0, 0.0).astype(BF16)
        sums = jnp.dot(product, keep, preferred_element_type=F32)
        out_ref[:, d * 128 : (d + 1) * 128] = sums.astype(BF16)
        turned = further


def lag_sums(form, band, own):
    return pl.pallas_call(
        partial(lag_sums_kernel, form, band),
        out_shape=jax.ShapeDtypeStruct((form.padded, 64 * 128), BF16),
        in_specs=[VMEM],
        out_specs=VMEM,
        compiler_params=params(12),
        cost_estimate=cost(2 * 10**9, 3 * 10**6),
        name="lag_sums",
    )(own)


def spectra_kernel(form, own_ref, forward_ref, to_weights_ref, inverse_ref, freq_ref, column_ref):
    window, windows = lax.axis_index("tm"), lax.axis_size("tm")
    rows = [own_rows(form, own_ref, band) for band in range(BANDS)]
    middle = jnp.concatenate([cells for cells, _ in rows], axis=0)
    rest = jnp.concatenate([left for _, left in rows], axis=0)
    dot = partial(jnp.dot, precision=HIGH, preferred_element_type=F32)
    forward = forward_ref[...]
    spectrum = dot(middle, forward_ref[0:128])
    low, high = spectrum[:, :128], spectrum[:, 128:]
    lane = iota(low.shape, 1)
    inner = jnp.where(lane == 0, 0.0, high)
    last = jnp.where(lane == 0, high, 0.0)
    strength = jnp.concatenate([low * low + inner * inner, last * last], axis=1)
    weights = dot(strength, to_weights_ref[...])
    place_in = iota((128, 256), 0) + iota((128, 256), 1)
    count = iota((128, 256), 1)
    outside = ((window == 0) & (place_in < LAG)) | (
        (window == windows - 1) & (place_in >= LAG + 128) & (count < NLAG)
    )
    outside = jnp.where(outside, 1.0, 0.0).astype(BF16)
    sums = jnp.dot(middle.astype(BF16), outside, preferred_element_type=F32)
    edge_sum = jnp.sum(sums * sums, axis=1, keepdims=True)
    other = dot(sums, forward)
    other_low, other_high = other[:, :128], other[:, 128:]
    cross = other_high * high
    real = other_low * low - jnp.where(lane == 0, 0.0, cross)
    imag = jnp.where(lane == 0, cross, other_low * high + other_high * low)
    edge = dot(jnp.concatenate([real, imag], axis=1), inverse_ref[...])
    factor = rest * (1.0 / (128 * 128 * NLAG))
    column = jnp.where(lane == 0, edge_sum, jnp.where(lane == 1, factor, 0.0))
    for band in range(BANDS):
        cut = slice(band * form.padded, (band + 1) * form.padded)
        big = weights[cut].astype(BF16)
        freq_ref[band, :, 0:256] = big
        freq_ref[band, :, 256:512] = (weights[cut] - big.astype(F32)).astype(BF16)
        freq_ref[band, :, 512:768] = big
        freq_ref[band, :, 768:1024] = edge[cut].astype(BF16)
        column_ref[band] = column[cut]


def spectra(form, own):
    shapes = [((BANDS, form.padded, 1024), BF16), ((BANDS, form.padded, 128), F32)]
    return pl.pallas_call(
        partial(spectra_kernel, form),
        out_shape=[jax.ShapeDtypeStruct(*shape) for shape in shapes],
        in_specs=[VMEM] * 4,
        out_specs=[VMEM] * 2,
        compiler_params=params(12),
        cost_estimate=cost(2 * 10**9, 2 * 10**6),
        name="row_spectra",
    )(own, jnp.asarray(FORWARD), jnp.asarray(TO_WEIGHTS), jnp.asarray(INVERSE))


def mean_column(form, block, at=0):
    shape = (form.padded, form.height - form.tail)
    row, col = iota(shape, 0), iota(shape, 1) - form.first
    pick = (col == row // 64) | (col - 16 == row // 64)
    pick = jnp.where(pick, 1.0, 0.0).astype(BF16)
    spread = jnp.dot(pick, block[form.tail :], preferred_element_type=F32)
    own = iota(spread.shape, 1) == lax.rem(iota(spread.shape, 0), 64) + at
    return jnp.sum(jnp.where(own, spread, 0.0), axis=1, keepdims=True)


def pieces(form, owners, owner):
    at = owner * form.rows
    found = []
    for lo, hi, gap in ((0, SPLIT, 0), (SPLIT, owners * form.rows, GROUP - SPLIT)):
        start, stop = max(lo, at), min(hi, at + form.rows)
        if start < stop:
            found.append((slice(start - at, stop - at), slice(start + gap, stop + gap)))
    return found


def stands(order, k):
    return sum(lax.rem(k // bit, 2) << j for j, bit in enumerate(order))


def gaps(form, owners):
    end = GROUP + owners * form.rows - SPLIT
    return (slice(SPLIT, GROUP), slice(end, columns_of(form, owners)))


def columns_of(form, owners):
    return GROUP + (owners * form.rows - SPLIT + TILE - 1) // TILE * TILE


def scaled_rows_kernel(form, owners, orders, near_0, far_0, near_1, far_1, middle_ref, extra_ref, blocks):
    me = lax.axis_index("vert")
    window, windows = lax.axis_index("tm"), lax.axis_size("tm")
    edge = (window == 0) | (window == windows - 1)
    half = owners // 2
    lane = iota((1, 128), 1)
    for band, (low, high) in enumerate(((near_0, far_0), (near_1, far_1))):
        blocks[0:half] = low[...]
        blocks[half:owners] = high[...]
        for cut in gaps(form, owners):
            middle_ref[band, cut] = jnp.zeros((cut.stop - cut.start, 128), F32)
            extra_ref[band, cut] = jnp.zeros((cut.stop - cut.start, 128), F32)
        for owner in range(owners):
            block = blocks[stands(orders[band], me ^ owner)]
            middle = block[0 : form.padded].astype(F32)
            mean = mean_column(form, block)
            power, left_over = scales_of(middle)
            mu = jnp.where(edge, mean.astype(BF16).astype(F32) * power, 0.0)
            scaled = middle * power
            extra = jnp.where(lane == 0, mu, jnp.where(lane == 1, left_over, jnp.where(lane == 2, power, mean)))
            for cut, put in pieces(form, owners, owner):
                middle_ref[band, put] = scaled[cut]
                extra_ref[band, put] = extra[cut]


def scaled_rows(form, owners, orders, *halves):
    shape = jax.ShapeDtypeStruct((BANDS, columns_of(form, owners), 128), F32)
    return pl.pallas_call(
        partial(scaled_rows_kernel, form, owners, orders),
        out_shape=[shape] * 2,
        in_specs=[VMEM] * len(halves),
        out_specs=[VMEM] * 2,
        scratch_shapes=[pltpu.VMEM((owners, form.height, 128), BF16)],
        compiler_params=params(12),
        cost_estimate=cost(10**9, 4 * 10**6),
        name="scaled_rows",
    )(*halves)


def margins_kernel(owners, *refs):
    halves, outs = refs[:BANDS], refs[BANDS:]
    odd = lax.rem(lax.axis_index("tm"), 2) == 1
    is_low = iota((1, 128), 1) < LAG
    for n in range(owners):
        zero, one = (halves[band][n].astype(F32) for band in range(BANDS))
        early = jnp.where(is_low, zero, pltpu.roll(one, 64, 1)).astype(BF16)
        late = jnp.where(is_low, pltpu.roll(zero, 64, 1), one).astype(BF16)
        outs[0][n] = jnp.where(odd, early, late)
        outs[1][n] = jnp.where(odd, late, early)


def margins(*halves):
    return pl.pallas_call(
        partial(margins_kernel, halves[0].shape[0]),
        out_shape=[jax.ShapeDtypeStruct(halves[0].shape, BF16)] * 2,
        in_specs=[VMEM] * len(halves),
        out_specs=[VMEM] * 2,
        compiler_params=params(8),
        cost_estimate=cost(10**6, 2 * 10**6),
        name="margins",
    )(*halves)


def coupling_kernel(
    form, owners, orders, lag_0, lag_1, freq_ref, column_ref, middle_ref, extra_ref,
    first_0, second_0, first_1, second_1, factor_ref, out_ref, result, first_ref, second_ref, around_rows, near, far, near_turn, far_turn, change
):
    me = lax.axis_index("vert")
    window, windows = lax.axis_index("tm"), lax.axis_size("tm")
    odd = lax.rem(window, 2) == 1
    half = owners // 2
    for whole, low, high in ((first_ref, first_0, first_1), (second_ref, second_0, second_1)):
        whole[0:half] = low[...]
        whole[half:owners] = high[...]
    result[...] = jnp.zeros_like(result)
    for cut in gaps(form, owners):
        around_rows[:, cut] = jnp.zeros((BANDS, cut.stop - cut.start, 128), F32)
    lane = iota((1, 128), 1)
    is_left = lane < LAG
    first_window, last_window = window == 0, window == windows - 1
    outside = (first_window & is_left) | (last_window & ~is_left)
    begin = me * form.rows
    end = jnp.minimum(begin + form.rows, SPLIT + P3)
    coarse, fine = begin < SPLIT, end > SPLIT
    for band in range(BANDS):
        for owner in range(owners):
            p = stands(orders[band], me ^ owner)
            one, two = first_ref[p], second_ref[p]
            left, right = jnp.where(odd, one, two), jnp.where(odd, two, one)
            shift_left = mean_column(form, left, band * 64)
            shift_right = mean_column(form, right, band * 64)
            left, right = (cells[0 : form.padded].astype(F32) for cells in (left, right))
            if band == 0:
                right = pltpu.roll(right, 64, 1)
            else:
                left = pltpu.roll(left, 64, 1)
            around = jnp.where(is_left, left + shift_left, right + shift_right)
            for cut, put in pieces(form, owners, owner):
                extra = extra_ref[band, put]
                shifted = (around[cut] - extra[:, 3:4]).astype(BF16).astype(F32) * extra[:, 2:3]
                around_rows[band, put] = jnp.where(outside, 0.0, shifted)

    own_parcel = iota((form.padded, 1), 0) + me * form.rows
    own_level = level_of(own_parcel)
    own_level = jnp.where(own_level < 3, own_level, -1)

    def tile(band, start, height, step, carry):
        lag_ref = (lag_0, lag_1)[band]
        rows_of = slice(start, start + height)
        first = pl.multiple_of(step * TILE, TILE)
        tile_of = pl.ds(first, TILE)
        columns = jnp.concatenate([middle_ref[band, tile_of].T, around_rows[band, tile_of].T], axis=0)
        constants = extra_ref[band, tile_of].T
        narrow = columns.astype(BF16)
        near[0:64] = columns[128:192]
        near[64:127] = columns[0:63]
        near[127:191] = columns[128:192]
        far[0:63] = columns[65:128]
        far[63:127] = columns[192:256]
        far[127:190] = columns[65:128]
        far[190:191] = columns[192:193]
        twice = jnp.concatenate([narrow, narrow], axis=0)
        spectra = jnp.dot(factor_ref[...], twice, preferred_element_type=F32)
        low_a, high_a, low_c, high_c = (spectra[128 * k : 128 * (k + 1)] for k in range(4))
        at_zero = iota((128, TILE), 0) == 0
        cross = high_a * high_c
        real = low_a * low_c + jnp.where(at_zero, 0.0, cross)
        imag = jnp.where(at_zero, cross, low_a * high_c - high_a * low_c)
        both = jnp.concatenate([real, imag], axis=0)
        big = both.astype(BF16)
        small = (both - big.astype(F32)).astype(BF16)
        mu, other_factor = constants[0:1], constants[1:2]
        mixed = (columns * (-2.0 * mu)).astype(BF16)
        for n, part in enumerate((big, big, small, mixed)):
            change[LAGS + 256 * n : LAGS + 256 * (n + 1)] = part
        for r in range(16):
            near_turn[r] = near[r : r + 176].astype(BF16)
            far_turn[r] = far[r : r + 176].astype(BF16)
        for d in range(64):
            a, r = divmod(d, 16)
            change[d * 128 : (d + 1) * 128] = (
                far_turn[0, 0:128] * far_turn[r, 16 * a : 16 * a + 128]
                - near_turn[0, 0:128] * near_turn[r, 16 * a : 16 * a + 128]
            )
        weights = jnp.concatenate([lag_ref[rows_of], freq_ref[band, rows_of]], axis=1)
        total = jnp.dot(weights, change[...], preferred_element_type=F32)
        factors = column_ref[band, rows_of]
        edge_sum, own_factor = factors[:, 0:1], factors[:, 1:2]
        total += mu * mu * edge_sum
        column = iota((1, TILE), 1) + first
        parcel = jnp.where(column < GROUP, column, column - (GROUP - SPLIT))
        gap = (column >= SPLIT) & (column < GROUP)
        other_level = jnp.where(gap, 3, level_of(parcel))
        scaled = total * own_factor * other_factor
        same = own_level[rows_of] == other_level
        result[band, rows_of, pl.ds(first, TILE)] = jnp.where(same, scaled, 0.0)
        return carry

    tiles = result.shape[2] // TILE
    fold = GROUP // TILE
    for band in range(BANDS):
        run = lambda lo, hi, start, height: lax.fori_loop(
            lo, hi, partial(tile, band, start, height), 0
        )
        low, high = jnp.where(coarse, 0, fold), jnp.where(fine, tiles, fold)
        cut = SPLIT % form.rows
        if form.padded - 128 <= cut <= 128:
            mixed = coarse & fine
            run(0, jnp.where(mixed, fold, 0), 0, 128)
            run(jnp.where(mixed, fold, tiles), tiles, form.padded - 128, 128)
            low = jnp.where(mixed, high, low)
        run(low, high, 0, form.padded)
    total = owners * form.rows
    for band in range(BANDS):
        out_ref[:, band, 0:SPLIT] = result[band, 0 : form.rows, 0:SPLIT]
        out_ref[:, band, SPLIT:total] = result[band, 0 : form.rows, GROUP : GROUP + total - SPLIT]


def coupling(form, owners, orders, *operands):
    total = owners * form.rows
    width = columns_of(form, owners)
    operands = (*operands, jnp.asarray(FACTORS))
    return pl.pallas_call(
        partial(coupling_kernel, form, owners, orders),
        out_shape=jax.ShapeDtypeStruct((form.rows, BANDS, total), F32),
        in_specs=[VMEM] * len(operands),
        out_specs=VMEM,
        scratch_shapes=[
            pltpu.VMEM((BANDS, form.padded, width), F32),
            pltpu.VMEM((owners, form.height, 128), BF16),
            pltpu.VMEM((owners, form.height, 128), BF16),
            pltpu.VMEM((BANDS, width, 128), F32),
            pltpu.VMEM((192, TILE), F32),
            pltpu.VMEM((192, TILE), F32),
            pltpu.VMEM((16, 176, TILE), BF16),
            pltpu.VMEM((16, 176, TILE), BF16),
            pltpu.VMEM((LAGS + 1024, TILE), BF16),
        ],
        compiler_params=params(24),
        cost_estimate=cost(16 * 10**9, 10**7),
        name="coupling",
    )(*operands)


def swap(cells, owners, bit):
    return lax.ppermute(cells, "vert", [(i, i ^ bit) for i in range(owners)])


def local(source, band_taps, smooth_taps, parcel_ids):
    vert_dev, t_dev = source.shape
    owners, windows = lax.axis_size("vert"), lax.axis_size("tm")
    form = Rows((P1 + P2 + P3 + owners - 1) // owners)
    bits = [1 << k for k in range(owners.bit_length() - 1)]
    orders = [bits, [bits[1], bits[0], *bits[2:]]]
    meet = [[p for i in range(k, windows - 1, 2) for p in ((i, i + 1), (i + 1, i))] for k in range(2)]
    first, second = (lax.ppermute(source, "tm", pairs) for pairs in meet)
    taps = jnp.concatenate([band_taps.reshape(2 * BANDS, TAPS), smooth_taps], axis=0).astype(F32)
    taps = jnp.pad(taps, ((0, 8 - 3 * BANDS), (0, 256 - TAPS)))
    prepared = prepare(form, owners, source, taps, parcel_ids)
    parts = front(form, owners, orders, first, second, *prepared)
    parts = [parts[0:2], parts[2:4]]
    for step in range(len(bits) - 1):
        arrived = [swap(parts[b][1], owners, orders[b][step]) for b in range(BANDS)]
        sums = [added(form, parts[b][0], arrived[b]) for b in range(BANDS)]
        half = sums[0].shape[0] // 2
        parts = [(cells[:half], cells[half:]) for cells in sums]
    kept, sent = (jnp.concatenate([parts[b][k] for b in range(BANDS)], axis=0) for k in range(2))
    theirs = swap(jnp.concatenate([kept, sent], axis=0), owners, bits[-1])
    both = added(form, jnp.concatenate([kept, sent], axis=0), jnp.concatenate([theirs[BANDS:], theirs[:BANDS]], axis=0))
    own = both[:BANDS]
    held = [jnp.stack([both[b], both[BANDS + b]]) for b in range(BANDS)]
    lag = [lag_sums(form, 0, own), None]
    sides = []

    def send_margins(packed):
        sides.append([lax.ppermute(cells, "tm", pairs) for cells, pairs in zip(packed, meet)])

    for step in range(len(bits) - 2, -1, -1):
        arrived = [swap(held[b], owners, orders[b][step]) for b in range(BANDS)]
        if step:
            held = [jnp.concatenate([held[b], arrived[b]], axis=0) for b in range(BANDS)]
            if step == 1:
                held, lag[0] = lax.optimization_barrier((held, lag[0]))
        else:
            packed, own = lax.optimization_barrier((margins(*held), own))
            send_margins(packed)
            lag[1] = lag_sums(form, 1, own)
            arrived, lag[1] = lax.optimization_barrier((arrived, lag[1]))
            packed, own = lax.optimization_barrier((margins(*arrived), own))
            send_margins(packed)
    freq, column = spectra(form, own)
    turned = [order[::-1] for order in orders]
    middle, extra = scaled_rows(form, owners, turned, held[0], arrived[0], held[1], arrived[1])
    done = coupling(form, owners, turned, *lag, freq, column, middle, extra, *sides[0], *sides[1])
    return done.transpose(1, 0, 2)[None]


def solution(mesh):
    return jax.shard_map(
        local,
        mesh=mesh,
        in_specs=(P("vert", "tm"), P(), P(), P(None, "vert")),
        out_specs=P("tm", None, "vert", None),
        check_vma=False,
    )
```

```python
from functools import partial

import numpy as np

import jax
import jax.numpy as jnp
from jax import lax
from jax.experimental import pallas as pl
from jax.experimental.pallas import tpu as pltpu
from jax.sharding import PartitionSpec as P

P1 = 100
P2 = 400
P3 = 1000
BANDS = 2
TAPS = 65
HALF = 32
LAG = 64
NLAG = 129
EPSILON = 1e-05
SPLIT = P1 + P2
GROUP = (SPLIT + 127) // 128 * 128
TILE = 256
PERIOD = 127
LAGS = 64 * 128
HIGH = lax.Precision.HIGHEST
BF16 = jnp.bfloat16
F32 = jnp.float32
VMEM = pl.BlockSpec(memory_space=pltpu.VMEM)


def fourier_constants():
    n = 256
    freq = np.arange(129)
    angle = 2 * np.pi * np.outer(np.arange(n), freq) / n
    cos, sin = np.cos(angle), np.sin(angle)
    weight = np.full(129, 2.0 / n)
    weight[[0, 128]] = 1.0 / n
    packed = np.concatenate([cos[:, :128], cos[:, 128:], -sin[:, 1:128]], axis=1)
    lags = np.arange(128)
    twice = np.where(lags == 0, 1.0, 2.0)
    from_power = weight[:, None] * cos[lags].T * twice
    scale = np.concatenate([weight[:128], weight[128:], weight[1:128]])
    to_weights = np.zeros((n, n))
    to_weights[:129] = (from_power @ packed[lags]) * scale
    order = np.concatenate([np.arange(64, 192), np.arange(0, 64), np.arange(192, 256)])
    inverse = (packed * scale).T[:, order]
    forward = packed * (np.arange(n) < NLAG)[:, None]
    near = forward.T[:, order]
    factors = np.concatenate([near, packed.T[:, order]], axis=0)
    high = factors.astype(np.float32).astype(jnp.bfloat16)
    low = (factors - high.astype(np.float64)).astype(np.float32).astype(jnp.bfloat16)
    f32 = lambda cells: cells.astype(np.float32)
    return f32(forward), f32(to_weights), f32(inverse), np.concatenate([high, low], axis=1)


FORWARD, TO_WEIGHTS, INVERSE, FACTORS = fourier_constants()


def params(mib):
    return pltpu.CompilerParams(vmem_limit_bytes=mib * 2**20)


def cost(flops, moved):
    return pl.CostEstimate(flops=flops, bytes_accessed=moved, transcendentals=0)


def iota(shape, dim):
    return lax.broadcasted_iota(jnp.int32, shape, dim)


class Rows:
    def __init__(self, par_dev):
        self.rows = par_dev
        self.padded = (par_dev + 15) // 16 * 16
        self.extra = (par_dev + 63) // 64
        self.tail = par_dev // 16 * 16
        self.first = par_dev - self.tail
        self.height = self.tail + 32
        assert 0 < self.first <= 16 - self.extra


def level_of(parcel):
    first = (parcel >= P1).astype(jnp.int32)
    second = (parcel >= SPLIT).astype(jnp.int32)
    third = (parcel >= SPLIT + P3).astype(jnp.int32)
    return first + second + third


def put_tail(form, tail, above, mean_rows):
    tail[...] = jnp.zeros_like(tail)
    tail[0 : form.first] = above
    high = mean_rows.astype(BF16).astype(F32)
    at = form.first
    tail[at : at + form.extra] = high
    tail[at + 16 : at + 16 + form.extra] = mean_rows - high
    return tail[...].astype(BF16)


def prepare_kernel(form, owners, middle_ref, taps_ref, ids_ref, source_ref, filter_ref, smoother_ref, hits_ref):
    me = lax.axis_index("vert")
    source_ref[...] = middle_ref[...]
    for k in range(2 * BANDS):
        taps = jnp.broadcast_to(taps_ref[k : k + 1], (256, 256))
        filter_ref[k] = pltpu.roll(taps, 192, 1, stride=1, stride_axis=0).astype(BF16)
    for k in range(BANDS):
        taps = jnp.broadcast_to(taps_ref[4 + k : 5 + k], (128, 256))
        smoother_ref[k] = pltpu.roll(taps, 0, 1, stride=1, stride_axis=0).astype(BF16)
    offsets = (0, P1, SPLIT)
    ids = [ids_ref[r : r + 1] + offsets[r] for r in range(3)]
    for k in range(owners):
        wanted = iota((form.padded, 1), 0) + (me ^ k) * form.rows
        hits = (wanted == ids[0]) | (wanted == ids[1]) | (wanted == ids[2])
        hits_ref[k] = jnp.where(hits, 1.0, 0.0).astype(BF16)


def prepare(form, owners, source, taps, ids):
    shapes = [source.shape, (2 * BANDS, 256, 256), (BANDS, 128, 256), (owners, form.padded, source.shape[0])]
    return pl.pallas_call(
        partial(prepare_kernel, form, owners),
        out_shape=[jax.ShapeDtypeStruct(shape, BF16) for shape in shapes],
        in_specs=[VMEM] * 3,
        out_specs=[VMEM] * 4,
        compiler_params=params(16),
        cost_estimate=cost(2 * 10**9, 5 * 10**6),
        name="prepare",
    )(source, taps, ids)


def front_kernel(form, owners, orders, first_ref, second_ref, middle_ref, filter_ref, smoother_ref, hits_ref, *rest):
    outs, (env, tail) = rest[: 2 * BANDS], rest[2 * BANDS :]
    filters = [filter_ref[k] for k in range(2 * BANDS)]
    smooths = [smoother_ref[k] for k in range(BANDS)]
    turned = (((1,), (1,)), ((), ()))
    vertices = middle_ref.shape[0]
    step = 256
    odd = lax.rem(lax.axis_index("tm"), 2) == 1
    for at in range(0, vertices, step):
        cut = slice(at, at + step)
        first, second = first_ref[cut], second_ref[cut]
        right = jnp.where(odd, second, first)[:, 0:64]
        left = jnp.where(odd, first, second)[:, 64:128]
        wide = jnp.concatenate([middle_ref[cut], right, left], axis=1)
        for band in range(BANDS):
            one = lax.dot_general(wide, filters[band], turned, preferred_element_type=F32)
            two = lax.dot_general(wide, filters[BANDS + band], turned, preferred_element_type=F32)
            power = (one * one + two * two).astype(BF16)
            smooth = lax.dot_general(power, smooths[band], turned, preferred_element_type=F32)
            env[cut, band * 128 : (band + 1) * 128] = smooth.astype(BF16)
    height = form.padded
    lane = iota((64, 128), 1)
    row = iota((64, 128), 0)
    diagonal = lax.rem(lane, 64) == row
    for k in range(owners):
        sums = jnp.dot(hits_ref[k], env[...], preferred_element_type=F32)
        for band in range(BANDS):
            cells = sums[:, band * 128 : (band + 1) * 128]
            mean = jnp.mean(cells, axis=1, keepdims=True)
            change = cells - mean
            means = jnp.concatenate(
                [
                    jnp.sum(
                        jnp.where(
                            diagonal[: min(64, height - 64 * e)], mean[64 * e : 64 * e + 64], 0.0
                        ),
                        axis=0,
                        keepdims=True,
                    )
                    for e in range(form.extra)
                ],
                axis=0,
            )
            p = place(k, orders[band][::-1])
            half = owners // 2
            out = outs[2 * band + p // half]
            out[p % half, 0 : form.tail] = change[0 : form.tail].astype(BF16)
            out[p % half, form.tail : form.height] = put_tail(
                form, tail, change[form.tail : form.rows], means
            )


def place(k, order):
    return sum((1 if k & bit else 0) << j for j, bit in enumerate(order))


def front(form, owners, orders, first, second, middle, *prepared):
    shape = jax.ShapeDtypeStruct((owners // 2, form.height, 128), BF16)
    operands = (first, second, middle, *prepared)
    return pl.pallas_call(
        partial(front_kernel, form, owners, orders),
        out_shape=[shape] * (2 * BANDS),
        in_specs=[VMEM] * len(operands),
        out_specs=[VMEM] * (2 * BANDS),
        scratch_shapes=[
            pltpu.VMEM((middle.shape[0], BANDS * 128), BF16),
            pltpu.VMEM((form.height - form.tail, 128), F32),
        ],
        compiler_params=params(16),
        cost_estimate=cost(3 * 10**9, 2 * 10**6),
        name="envelope_sums",
    )(*operands)


def added(form, kept, arrived):
    whole = kept.astype(F32) + arrived.astype(F32)
    high, low = whole[:, form.tail : form.tail + 16], whole[:, form.tail + 16 :]
    row = lax.broadcasted_iota(jnp.int32, high.shape, 1)
    holds = (row >= form.first) & (row < form.first + form.extra)
    mean = high + low
    big = lax.reduce_precision(mean, 8, 7)
    parts = [whole[:, : form.tail], jnp.where(holds, big, high), jnp.where(holds, mean - big, 0.0)]
    return jnp.concatenate([part.astype(BF16) for part in parts], axis=1)


def scales_of(middle):
    spread = lax.rsqrt(jnp.mean(middle * middle, axis=1, keepdims=True) + EPSILON)
    power = jnp.exp2(jnp.floor(jnp.log2(spread)))
    rest = spread / power
    return power, rest * rest


def own_rows(form, own_ref, band):
    middle = own_ref[band, 0 : form.padded].astype(F32)
    middle = jnp.where(iota(middle.shape, 0) < form.rows, middle, 0.0)
    power, rest = scales_of(middle)
    return middle * power, rest


def lag_sums_kernel(form, band, own_ref, out_ref):
    middle = own_rows(form, own_ref, band)[0]
    lane = iota((1, 128), 1)
    row = iota((128, 128), 0)
    col = iota((128, 128), 1)
    turned = middle
    for d in range(64):
        further = pltpu.roll(middle, PERIOD - d, 1)
        partner = jnp.where(lane <= PERIOD - d, turned, further)
        product = (middle * partner).astype(BF16)
        keep = (row > col) & ((row <= PERIOD - d) == (col < PERIOD - d))
        keep = jnp.where(keep, 2.0 if d else 1.0, 0.0).astype(BF16)
        sums = jnp.dot(product, keep, preferred_element_type=F32)
        out_ref[:, d * 128 : (d + 1) * 128] = sums.astype(BF16)
        turned = further


def lag_sums(form, band, own):
    return pl.pallas_call(
        partial(lag_sums_kernel, form, band),
        out_shape=jax.ShapeDtypeStruct((form.padded, 64 * 128), BF16),
        in_specs=[VMEM],
        out_specs=VMEM,
        compiler_params=params(12),
        cost_estimate=cost(2 * 10**9, 3 * 10**6),
        name="lag_sums",
    )(own)


def spectra_kernel(form, own_ref, forward_ref, to_weights_ref, inverse_ref, freq_ref, column_ref):
    window, windows = lax.axis_index("tm"), lax.axis_size("tm")
    rows = [own_rows(form, own_ref, band) for band in range(BANDS)]
    middle = jnp.concatenate([cells for cells, _ in rows], axis=0)
    rest = jnp.concatenate([left for _, left in rows], axis=0)
    dot = partial(jnp.dot, precision=HIGH, preferred_element_type=F32)
    forward = forward_ref[...]
    spectrum = dot(middle, forward_ref[0:128])
    low, high = spectrum[:, :128], spectrum[:, 128:]
    lane = iota(low.shape, 1)
    inner = jnp.where(lane == 0, 0.0, high)
    last = jnp.where(lane == 0, high, 0.0)
    strength = jnp.concatenate([low * low + inner * inner, last * last], axis=1)
    weights = dot(strength, to_weights_ref[...])
    place_in = iota((128, 256), 0) + iota((128, 256), 1)
    count = iota((128, 256), 1)
    outside = ((window == 0) & (place_in < LAG)) | (
        (window == windows - 1) & (place_in >= LAG + 128) & (count < NLAG)
    )
    outside = jnp.where(outside, 1.0, 0.0).astype(BF16)
    sums = jnp.dot(middle.astype(BF16), outside, preferred_element_type=F32)
    edge_sum = jnp.sum(sums * sums, axis=1, keepdims=True)
    other = dot(sums, forward)
    other_low, other_high = other[:, :128], other[:, 128:]
    cross = other_high * high
    real = other_low * low - jnp.where(lane == 0, 0.0, cross)
    imag = jnp.where(lane == 0, cross, other_low * high + other_high * low)
    edge = dot(jnp.concatenate([real, imag], axis=1), inverse_ref[...])
    factor = rest * (1.0 / (128 * 128 * NLAG))
    column = jnp.where(lane == 0, edge_sum, jnp.where(lane == 1, factor, 0.0))
    for band in range(BANDS):
        cut = slice(band * form.padded, (band + 1) * form.padded)
        big = weights[cut].astype(BF16)
        freq_ref[band, :, 0:256] = big
        freq_ref[band, :, 256:512] = (weights[cut] - big.astype(F32)).astype(BF16)
        freq_ref[band, :, 512:768] = big
        freq_ref[band, :, 768:1024] = edge[cut].astype(BF16)
        column_ref[band] = column[cut]


def spectra(form, own):
    shapes = [((BANDS, form.padded, 1024), BF16), ((BANDS, form.padded, 128), F32)]
    return pl.pallas_call(
        partial(spectra_kernel, form),
        out_shape=[jax.ShapeDtypeStruct(*shape) for shape in shapes],
        in_specs=[VMEM] * 4,
        out_specs=[VMEM] * 2,
        compiler_params=params(12),
        cost_estimate=cost(2 * 10**9, 2 * 10**6),
        name="row_spectra",
    )(own, jnp.asarray(FORWARD), jnp.asarray(TO_WEIGHTS), jnp.asarray(INVERSE))


def mean_column(form, block, at=0):
    shape = (form.padded, form.height - form.tail)
    row, col = iota(shape, 0), iota(shape, 1) - form.first
    pick = (col == row // 64) | (col - 16 == row // 64)
    pick = jnp.where(pick, 1.0, 0.0).astype(BF16)
    spread = jnp.dot(pick, block[form.tail :], preferred_element_type=F32)
    own = iota(spread.shape, 1) == lax.rem(iota(spread.shape, 0), 64) + at
    return jnp.sum(jnp.where(own, spread, 0.0), axis=1, keepdims=True)


def pieces(form, owners, owner):
    at = owner * form.rows
    found = []
    for lo, hi, gap in ((0, SPLIT, 0), (SPLIT, owners * form.rows, GROUP - SPLIT)):
        start, stop = max(lo, at), min(hi, at + form.rows)
        if start < stop:
            found.append((slice(start - at, stop - at), slice(start + gap, stop + gap)))
    return found


def stands(order, k):
    return sum(lax.rem(k // bit, 2) << j for j, bit in enumerate(order))


def gaps(form, owners):
    end = GROUP + owners * form.rows - SPLIT
    return (slice(SPLIT, GROUP), slice(end, columns_of(form, owners)))


def columns_of(form, owners):
    return GROUP + (owners * form.rows - SPLIT + TILE - 1) // TILE * TILE


def scaled_rows_kernel(form, owners, orders, near_0, far_0, near_1, far_1, middle_ref, extra_ref, blocks):
    me = lax.axis_index("vert")
    window, windows = lax.axis_index("tm"), lax.axis_size("tm")
    edge = (window == 0) | (window == windows - 1)
    half = owners // 2
    lane = iota((1, 128), 1)
    for band, (low, high) in enumerate(((near_0, far_0), (near_1, far_1))):
        blocks[0:half] = low[...]
        blocks[half:owners] = high[...]
        for cut in gaps(form, owners):
            middle_ref[band, cut] = jnp.zeros((cut.stop - cut.start, 128), F32)
            extra_ref[band, cut] = jnp.zeros((cut.stop - cut.start, 128), F32)
        for owner in range(owners):
            block = blocks[stands(orders[band], me ^ owner)]
            middle = block[0 : form.padded].astype(F32)
            mean = mean_column(form, block)
            power, left_over = scales_of(middle)
            mu = jnp.where(edge, mean.astype(BF16).astype(F32) * power, 0.0)
            scaled = middle * power
            extra = jnp.where(lane == 0, mu, jnp.where(lane == 1, left_over, jnp.where(lane == 2, power, mean)))
            for cut, put in pieces(form, owners, owner):
                middle_ref[band, put] = scaled[cut]
                extra_ref[band, put] = extra[cut]


def scaled_rows(form, owners, orders, *halves):
    shape = jax.ShapeDtypeStruct((BANDS, columns_of(form, owners), 128), F32)
    return pl.pallas_call(
        partial(scaled_rows_kernel, form, owners, orders),
        out_shape=[shape] * 2,
        in_specs=[VMEM] * len(halves),
        out_specs=[VMEM] * 2,
        scratch_shapes=[pltpu.VMEM((owners, form.height, 128), BF16)],
        compiler_params=params(12),
        cost_estimate=cost(10**9, 4 * 10**6),
        name="scaled_rows",
    )(*halves)


def margins_kernel(owners, *refs):
    halves, outs = refs[:BANDS], refs[BANDS:]
    odd = lax.rem(lax.axis_index("tm"), 2) == 1
    is_low = iota((1, 128), 1) < LAG
    for n in range(owners):
        zero, one = (halves[band][n].astype(F32) for band in range(BANDS))
        early = jnp.where(is_low, zero, pltpu.roll(one, 64, 1)).astype(BF16)
        late = jnp.where(is_low, pltpu.roll(zero, 64, 1), one).astype(BF16)
        outs[0][n] = jnp.where(odd, early, late)
        outs[1][n] = jnp.where(odd, late, early)


def margins(*halves):
    return pl.pallas_call(
        partial(margins_kernel, halves[0].shape[0]),
        out_shape=[jax.ShapeDtypeStruct(halves[0].shape, BF16)] * 2,
        in_specs=[VMEM] * len(halves),
        out_specs=[VMEM] * 2,
        compiler_params=params(8),
        cost_estimate=cost(10**6, 2 * 10**6),
        name="margins",
    )(*halves)


def coupling_kernel(
    form, owners, orders, lag_0, lag_1, freq_ref, column_ref, middle_ref, extra_ref,
    first_0, second_0, first_1, second_1, factor_ref, out_ref, result, first_ref, second_ref, around_rows, near, far, near_turn, far_turn, change
):
    me = lax.axis_index("vert")
    window, windows = lax.axis_index("tm"), lax.axis_size("tm")
    odd = lax.rem(window, 2) == 1
    half = owners // 2
    for whole, low, high in ((first_ref, first_0, first_1), (second_ref, second_0, second_1)):
        whole[0:half] = low[...]
        whole[half:owners] = high[...]
    result[...] = jnp.zeros_like(result)
    for cut in gaps(form, owners):
        around_rows[:, cut] = jnp.zeros((BANDS, cut.stop - cut.start, 128), F32)
    lane = iota((1, 128), 1)
    is_left = lane < LAG
    first_window, last_window = window == 0, window == windows - 1
    outside = (first_window & is_left) | (last_window & ~is_left)
    begin = me * form.rows
    end = jnp.minimum(begin + form.rows, SPLIT + P3)
    coarse, fine = begin < SPLIT, end > SPLIT
    for band in range(BANDS):
        for owner in range(owners):
            p = stands(orders[band], me ^ owner)
            one, two = first_ref[p], second_ref[p]
            left, right = jnp.where(odd, one, two), jnp.where(odd, two, one)
            shift_left = mean_column(form, left, band * 64)
            shift_right = mean_column(form, right, band * 64)
            left, right = (cells[0 : form.padded].astype(F32) for cells in (left, right))
            if band == 0:
                right = pltpu.roll(right, 64, 1)
            else:
                left = pltpu.roll(left, 64, 1)
            around = jnp.where(is_left, left + shift_left, right + shift_right)
            for cut, put in pieces(form, owners, owner):
                extra = extra_ref[band, put]
                shifted = (around[cut] - extra[:, 3:4]).astype(BF16).astype(F32) * extra[:, 2:3]
                around_rows[band, put] = jnp.where(outside, 0.0, shifted)

    own_parcel = iota((form.padded, 1), 0) + me * form.rows
    own_level = level_of(own_parcel)
    own_level = jnp.where(own_level < 3, own_level, -1)

    def tile(band, start, height, step, carry):
        lag_ref = (lag_0, lag_1)[band]
        rows_of = slice(start, start + height)
        first = pl.multiple_of(step * TILE, TILE)
        tile_of = pl.ds(first, TILE)
        columns = jnp.concatenate([middle_ref[band, tile_of].T, around_rows[band, tile_of].T], axis=0)
        constants = extra_ref[band, tile_of].T
        narrow = columns.astype(BF16)
        near[0:64] = columns[128:192]
        near[64:127] = columns[0:63]
        near[127:191] = columns[128:192]
        far[0:63] = columns[65:128]
        far[63:127] = columns[192:256]
        far[127:190] = columns[65:128]
        far[190:191] = columns[192:193]
        twice = jnp.concatenate([narrow, narrow], axis=0)
        spectra = jnp.dot(factor_ref[...], twice, preferred_element_type=F32)
        low_a, high_a, low_c, high_c = (spectra[128 * k : 128 * (k + 1)] for k in range(4))
        at_zero = iota((128, TILE), 0) == 0
        cross = high_a * high_c
        real = low_a * low_c + jnp.where(at_zero, 0.0, cross)
        imag = jnp.where(at_zero, cross, low_a * high_c - high_a * low_c)
        both = jnp.concatenate([real, imag], axis=0)
        big = both.astype(BF16)
        small = (both - big.astype(F32)).astype(BF16)
        mu, other_factor = constants[0:1], constants[1:2]
        mixed = (columns * (-2.0 * mu)).astype(BF16)
        for n, part in enumerate((big, big, small, mixed)):
            change[LAGS + 256 * n : LAGS + 256 * (n + 1)] = part
        for r in range(16):
            near_turn[r] = near[r : r + 176].astype(BF16)
            far_turn[r] = far[r : r + 176].astype(BF16)
        for h in (0, 64):
            far_0, near_0 = far_turn[0, h : h + 64], near_turn[0, h : h + 64]
            for d in range(64):
                a, r = divmod(d, 16)
                shift = slice(16 * a + h, 16 * a + h + 64)
                change[d * 128 + h : d * 128 + h + 64] = (
                    far_0 * far_turn[r, shift] - near_0 * near_turn[r, shift]
                )
        weights = jnp.concatenate([lag_ref[rows_of], freq_ref[band, rows_of]], axis=1)
        total = jnp.dot(weights, change[...], preferred_element_type=F32)
        factors = column_ref[band, rows_of]
        edge_sum, own_factor = factors[:, 0:1], factors[:, 1:2]
        total += mu * mu * edge_sum
        column = iota((1, TILE), 1) + first
        parcel = jnp.where(column < GROUP, column, column - (GROUP - SPLIT))
        gap = (column >= SPLIT) & (column < GROUP)
        other_level = jnp.where(gap, 3, level_of(parcel))
        scaled = total * own_factor * other_factor
        same = own_level[rows_of] == other_level
        result[band, rows_of, pl.ds(first, TILE)] = jnp.where(same, scaled, 0.0)
        return carry

    tiles = result.shape[2] // TILE
    fold = GROUP // TILE
    for band in range(BANDS):
        run = lambda lo, hi, start, height: lax.fori_loop(
            lo, hi, partial(tile, band, start, height), 0
        )
        low, high = jnp.where(coarse, 0, fold), jnp.where(fine, tiles, fold)
        cut = SPLIT % form.rows
        if form.padded > 128 and cut:
            mixed = coarse & fine
            run(0, jnp.where(mixed, fold, 0), 0, (cut + 31) // 32 * 32)
            upper = cut // 32 * 32
            run(jnp.where(mixed, fold, tiles), tiles, upper, form.padded - upper)
            low = jnp.where(mixed, high, low)
        run(low, high, 0, form.padded)
    total = owners * form.rows
    for band in range(BANDS):
        out_ref[:, band, 0:SPLIT] = result[band, 0 : form.rows, 0:SPLIT]
        out_ref[:, band, SPLIT:total] = result[band, 0 : form.rows, GROUP : GROUP + total - SPLIT]


def coupling(form, owners, orders, *operands):
    total = owners * form.rows
    width = columns_of(form, owners)
    operands = (*operands, jnp.asarray(FACTORS))
    return pl.pallas_call(
        partial(coupling_kernel, form, owners, orders),
        out_shape=jax.ShapeDtypeStruct((form.rows, BANDS, total), F32),
        in_specs=[VMEM] * len(operands),
        out_specs=VMEM,
        scratch_shapes=[
            pltpu.VMEM((BANDS, form.padded, width), F32),
            pltpu.VMEM((owners, form.height, 128), BF16),
            pltpu.VMEM((owners, form.height, 128), BF16),
            pltpu.VMEM((BANDS, width, 128), F32),
            pltpu.VMEM((192, TILE), F32),
            pltpu.VMEM((192, TILE), F32),
            pltpu.VMEM((16, 176, TILE), BF16),
            pltpu.VMEM((16, 176, TILE), BF16),
            pltpu.VMEM((LAGS + 1024, TILE), BF16),
        ],
        compiler_params=params(24),
        cost_estimate=cost(16 * 10**9, 10**7),
        name="coupling",
    )(*operands)


def swap(cells, owners, bit):
    return lax.ppermute(cells, "vert", [(i, i ^ bit) for i in range(owners)])


def local(source, band_taps, smooth_taps, parcel_ids):
    vert_dev, t_dev = source.shape
    owners, windows = lax.axis_size("vert"), lax.axis_size("tm")
    form = Rows((P1 + P2 + P3 + owners - 1) // owners)
    bits = [1 << k for k in range(owners.bit_length() - 1)]
    orders = [bits, [bits[1], bits[0], *bits[2:]]]
    meet = [[p for i in range(k, windows - 1, 2) for p in ((i, i + 1), (i + 1, i))] for k in range(2)]
    first, second = (lax.ppermute(source, "tm", pairs) for pairs in meet)
    taps = jnp.concatenate([band_taps.reshape(2 * BANDS, TAPS), smooth_taps], axis=0).astype(F32)
    taps = jnp.pad(taps, ((0, 8 - 3 * BANDS), (0, 256 - TAPS)))
    prepared = prepare(form, owners, source, taps, parcel_ids)
    parts = front(form, owners, orders, first, second, *prepared)
    parts = [parts[0:2], parts[2:4]]
    for step in range(len(bits) - 1):
        arrived = [swap(parts[b][1], owners, orders[b][step]) for b in range(BANDS)]
        sums = [added(form, parts[b][0], arrived[b]) for b in range(BANDS)]
        half = sums[0].shape[0] // 2
        parts = [(cells[:half], cells[half:]) for cells in sums]
    kept, sent = (jnp.concatenate([parts[b][k] for b in range(BANDS)], axis=0) for k in range(2))
    theirs = swap(jnp.concatenate([kept, sent], axis=0), owners, bits[-1])
    both = added(form, jnp.concatenate([kept, sent], axis=0), jnp.concatenate([theirs[BANDS:], theirs[:BANDS]], axis=0))
    own = both[:BANDS]
    held = [jnp.stack([both[b], both[BANDS + b]]) for b in range(BANDS)]
    lag = [lag_sums(form, 0, own), None]
    sides = []

    def send_margins(packed):
        sides.append([lax.ppermute(cells, "tm", pairs) for cells, pairs in zip(packed, meet)])

    for step in range(len(bits) - 2, -1, -1):
        arrived = [swap(held[b], owners, orders[b][step]) for b in range(BANDS)]
        if step:
            held = [jnp.concatenate([held[b], arrived[b]], axis=0) for b in range(BANDS)]
            if step == 1:
                held, lag[0] = lax.optimization_barrier((held, lag[0]))
        else:
            packed, own = lax.optimization_barrier((margins(*held), own))
            send_margins(packed)
            lag[1] = lag_sums(form, 1, own)
            arrived, lag[1] = lax.optimization_barrier((arrived, lag[1]))
            packed, own = lax.optimization_barrier((margins(*arrived), own))
            send_margins(packed)
    freq, column = spectra(form, own)
    turned = [order[::-1] for order in orders]
    middle, extra = scaled_rows(form, owners, turned, held[0], arrived[0], held[1], arrived[1])
    done = coupling(form, owners, turned, *lag, freq, column, middle, extra, *sides[0], *sides[1])
    return done.transpose(1, 0, 2)[None]


def solution(mesh):
    return jax.shard_map(
        local,
        mesh=mesh,
        in_specs=(P("vert", "tm"), P(), P(), P(None, "vert")),
        out_specs=P("tm", None, "vert", None),
        check_vma=False,
    )
```
